128 devices in a mesh: expert: 16 (over x, z), dp: 8 (over y, core).
Axes of the slice: x: 4, y: 4, z: 4, core: 2. Of those that a mesh axis runs over, the one named last changes fastest.
Arguments:
- tokens: bfloat16 [20480, 2048], P(('expert', 'dp')), may hold values from -6 to 6
- expert_ids: int32 [20480, 2], P(('expert', 'dp')), may hold values from 0 to 63, as said below
- gate_weights: float32 [20480, 2], P(('expert', 'dp')), may hold values from 0.1 to 1
- grad_output: bfloat16 [20480, 2048], P(('expert', 'dp')), may hold values from -6 to 6
- gate_weight: bfloat16 [128, 768, 2048], P(('expert', 'dp')), may hold values from -0.125 to 0.125
- up_weight: bfloat16 [128, 768, 2048], P(('expert', 'dp')), may hold values from -0.125 to 0.125
- down_weight: bfloat16 [128, 768, 2048], P(('expert', 'dp')), may hold values from -0.15625 to 0.15625
- swap_slot: int32 [8], replicated, may hold values from 0 to 3
- slot_cap: int32 [16, 4], replicated, may hold values from 2 to 5
Outputs:
- layer_out: bfloat16 [20480, 2048], P(('expert', 'dp'))
- grad_tokens: bfloat16 [20480, 2048], P(('expert', 'dp'))
- grad_routing: float32 [20480, 2], P(('expert', 'dp'))
- gate_grad: bfloat16 [128, 768, 2048], P(('expert', 'dp'))
- up_grad: bfloat16 [128, 768, 2048], P(('expert', 'dp'))
- down_grad: bfloat16 [128, 768, 2048], P(('expert', 'dp'))
The draws below stay inside these ranges and needn't reach their ends.
Inputs may be any that keep to these rules, and one draw needn't show every extreme that they name: `expert_ids`: in the rows of one device (aligned blocks of 160 rows) each expert is named by exactly 5 rows, and each row names 2 different experts.
All inputs are finite; a program needn't handle non-finite values.
Results may differ from the reference program's by a relative error of at most 0.0071.
Values may be sent and summed in bfloat16 or wider, within the bound.
A program may use at most 128 MiB of HBM per device.

```python
import math
import jax
import jax.numpy as jnp
from jax import lax

D = 2048
FF = 1536
SPLIT = 2
TOP = 2
TOK_DEV = 160
EXP_DEV = 4
EXPERTS = 64
CAP = 5
FF_HALF = 768
TOKENS = 20480
N_EXPERT = 16
N_DP = 8


def draw_slot_cap(key, part):
    key = jax.random.fold_in(key, 23)
    first_key, second_key = jax.random.split(key, 2)
    values = jax.random.randint(first_key, (N_EXPERT * EXP_DEV,), 2, CAP + 1)
    order = jax.random.permutation(second_key, N_EXPERT * EXP_DEV)
    values = values.at[order[0]].set(CAP).at[order[1]].set(2)
    return values.reshape(N_EXPERT, EXP_DEV).astype(jnp.int32)


def shuffle_rows(row_keys, listing):
    return jax.vmap(lambda one_key, one_row: jax.random.permutation(one_key, one_row))(row_keys, listing)


def deal_block(block_key):
    order_key, column_key, within_key = jax.random.split(block_key, 3)
    expert_order = jax.random.permutation(order_key, EXPERTS)
    dealt = expert_order[jnp.arange(TOK_DEV * TOP, dtype=jnp.int32) // CAP].reshape(TOP, TOK_DEV)
    columns = shuffle_rows(jax.random.split(column_key, TOP), dealt)
    listing = columns.T
    return shuffle_rows(jax.random.split(within_key, TOK_DEV), listing)


def draw_expert_ids(key, part):
    key = jax.random.fold_in(key, 41)
    block_keys = jax.random.split(key, N_EXPERT * N_DP)
    listing = jax.vmap(deal_block)(block_keys)
    return listing.reshape(TOKENS, TOP).astype(jnp.int32)


def with_ends(result, rng, low, largest):
    index_at = [jax.random.randint(jax.random.fold_in(rng, axis), (), 0, length) for axis, length in enumerate(result.shape)]
    main_axis = result.shape.index(max(result.shape))
    next_to = index_at[:main_axis] + [(index_at[main_axis] + 1) % result.shape[main_axis]] + index_at[main_axis + 1:]
    return result.at[tuple(index_at)].set(low).at[tuple(next_to)].set(largest)


def level_of(rng, dims, shards, low, largest):
    level, own = 1.0, jax.random.fold_in(rng, 6)
    for axis_at, parts in shards:
        steps = jnp.exp(jax.random.uniform(jax.random.fold_in(own, axis_at), (parts,), jnp.float32, low / len(shards), largest / len(shards)))
        level = level * jnp.repeat(steps, dims[axis_at] // parts).reshape([-1 if axis == axis_at else 1 for axis in range(len(dims))])
    return level


def scatter_about(rng, extent, spread, limit, pieces=(), kind=jnp.bfloat16):
    result = jax.random.normal(rng, extent, jnp.float32) * spread
    if len(pieces) > 0:
        result = level_of(rng, extent, pieces, -0.22, 0.18) * result
    return jnp.clip(result, min=-limit, max=limit).astype(kind)


def setup_inputs(seed: int = 0) -> dict:
    keys = jax.random.split(jax.random.key(seed), 10)
    return {
        "tokens": scatter_about(keys[0], (TOKENS, D), 1.0, 6.0, ((0, 128),)),
        "expert_ids": draw_expert_ids(jax.random.fold_in(keys[9], 71), 0),
        "gate_weights": jnp.clip(jnp.exp(math.log(1.0) - 2.3025851 * jax.random.uniform(keys[2], (TOKENS, TOP), jnp.float32) ** level_of(keys[2], (TOKENS, TOP), ((0, 128),), -0.2, 0.2)), 0.1, 1.0),
        "grad_output": scatter_about(keys[3], (TOKENS, D), 1.0, 6.0, ((0, 128),)),
        "gate_weight": scatter_about(keys[4], (EXPERTS * SPLIT, FF_HALF, D), D ** -0.5, 0.125, ((0, 128),)),
        "up_weight": scatter_about(keys[5], (EXPERTS * SPLIT, FF_HALF, D), D ** -0.5, 0.125, ((0, 128),)),
        "down_weight": scatter_about(keys[6], (EXPERTS * SPLIT, FF_HALF, D), FF ** -0.5, 0.15625, ((0, 128),)),
        "swap_slot": with_ends(jax.random.randint(keys[7], (N_EXPERT // 2,), 0, EXP_DEV), jax.random.fold_in(keys[7], 1), 0, EXP_DEV - 1).astype(jnp.int32),
        "slot_cap": draw_slot_cap(jax.random.fold_in(keys[9], 71), 0),
    }


def expert_pass(tokens, flat_gates, grad_output, gate_block, up_block, down_block, assigned):
    block_units = FF // SPLIT
    is_used = assigned >= 0
    safe_index = jnp.where(is_used, assigned, 0)
    token_at = safe_index // TOP
    token_rows = jnp.where(is_used[:, None], tokens[token_at], jnp.zeros((), tokens.dtype))
    scaled = flat_gates[safe_index][:, None] * grad_output[token_at].astype(jnp.float32)
    grads_in = jnp.where(is_used[:, None], scaled, 0.0).astype(jnp.bfloat16)
    gate_pre = jnp.dot(token_rows, gate_block.T, preferred_element_type=jnp.float32)
    up_pre = jnp.dot(token_rows, up_block.T, preferred_element_type=jnp.float32)
    activation = (jax.nn.silu(gate_pre) * up_pre).astype(jnp.bfloat16)
    act_blocks = activation.astype(jnp.float32).reshape(-1, SPLIT, block_units)
    down_blocks = down_block.astype(jnp.float32).reshape(SPLIT, block_units, D)
    partial_out = jnp.einsum("rnf,nfd->rnd", act_blocks, down_blocks)
    rounded_out = lax.optimization_barrier(partial_out.astype(jnp.bfloat16))
    out_rows = jnp.sum(rounded_out.astype(jnp.float32), axis=1).astype(jnp.bfloat16)
    grad_act = jnp.dot(grads_in, down_block.T, preferred_element_type=jnp.float32)
    down_result = jnp.dot(activation.T, grads_in, preferred_element_type=jnp.float32).astype(jnp.bfloat16)
    gate_sig = jax.nn.sigmoid(gate_pre)
    delta_gate = (grad_act * up_pre * gate_sig * (1.0 + gate_pre * (1.0 - gate_sig))).astype(jnp.bfloat16)
    delta_up = (grad_act * gate_pre * gate_sig).astype(jnp.bfloat16)
    gate_result = jnp.dot(delta_gate.T, token_rows, preferred_element_type=jnp.float32).astype(jnp.bfloat16)
    up_result = jnp.dot(delta_up.T, token_rows, preferred_element_type=jnp.float32).astype(jnp.bfloat16)
    gate_split = gate_block.astype(jnp.float32).reshape(SPLIT, block_units, D)
    up_split = up_block.astype(jnp.float32).reshape(SPLIT, block_units, D)
    dgate_split = delta_gate.astype(jnp.float32).reshape(-1, SPLIT, block_units)
    dup_split = delta_up.astype(jnp.float32).reshape(-1, SPLIT, block_units)
    partial_in = jnp.einsum("rnf,nfd->rnd", dgate_split, gate_split) + jnp.einsum("rnf,nfd->rnd", dup_split, up_split)
    rounded_in = lax.optimization_barrier(partial_in.astype(jnp.bfloat16))
    in_rows = jnp.sum(rounded_in.astype(jnp.float32), axis=1).astype(jnp.bfloat16)
    return out_rows, in_rows, gate_result, up_result, down_result


def reference(tokens, expert_ids, gate_weights, grad_output, gate_weight, up_weight, down_weight, swap_slot, slot_cap):
    half_axis = N_EXPERT // 2
    expert_range = jnp.arange(EXPERTS, dtype=jnp.int32)
    home_device = expert_range // EXP_DEV
    local_slot = expert_range % EXP_DEV
    was_moved = local_slot == swap_slot[home_device % half_axis]
    holder = jnp.where(was_moved, (home_device + half_axis) % N_EXPERT, home_device)
    capacity_of = slot_cap[holder, local_slot]
    source_count = N_EXPERT * N_DP
    assign_count = TOK_DEV * TOP
    routed_ids = expert_ids.reshape(source_count, assign_count)
    one_hot = (routed_ids[:, :, None] == expert_range[None, None, :]).astype(jnp.int32)
    rank_in = jnp.sum((jnp.cumsum(one_hot, axis=1) - one_hot) * one_hot, axis=2)
    is_kept = rank_in < capacity_of[routed_ids]
    source_ids = jnp.broadcast_to(jnp.arange(source_count, dtype=jnp.int32)[:, None], routed_ids.shape)
    flat_assign = source_ids * assign_count + jnp.arange(assign_count, dtype=jnp.int32)[None, :]
    slot_table = jnp.full((EXPERTS, source_count, CAP), -1, jnp.int32)
    slot_table = slot_table.at[routed_ids, source_ids, rank_in].set(jnp.where(is_kept, flat_assign, -1), mode="drop")
    slot_table = slot_table.reshape(EXPERTS, source_count * CAP)
    flat_gates = gate_weights.reshape(-1)
    gate_full = gate_weight.reshape(EXPERTS, FF, D)
    up_full = up_weight.reshape(EXPERTS, FF, D)
    down_full = down_weight.reshape(EXPERTS, FF, D)

    def per_expert(inputs):
        return expert_pass(tokens, flat_gates, grad_output, inputs[0], inputs[1], inputs[2], inputs[3])

    out_rows, in_rows, gate_grad, up_grad, down_grad = lax.map(per_expert, (gate_full, up_full, down_full, slot_table))
    flat_slots = slot_table.reshape(-1)
    target = jnp.where(flat_slots >= 0, flat_slots, source_count * assign_count)
    empty = jnp.zeros((source_count * assign_count, D), jnp.float32)
    out_assign = empty.at[target].set(out_rows.reshape(-1, D).astype(jnp.float32), mode="drop").reshape(TOKENS, TOP, D)
    in_assign = empty.at[target].set(in_rows.reshape(-1, D).astype(jnp.float32), mode="drop").reshape(TOKENS, TOP, D)
    layer_out = jnp.sum(gate_weights[:, :, None] * out_assign, axis=1).astype(jnp.bfloat16)
    grad_tokens = jnp.sum(in_assign, axis=1).astype(jnp.bfloat16)
    grad_routing = jnp.sum(grad_output.astype(jnp.float32)[:, None, :] * out_assign, axis=2)
    gate_grad = gate_grad.reshape(EXPERTS * SPLIT, FF // SPLIT, D)
    up_grad = up_grad.reshape(EXPERTS * SPLIT, FF // SPLIT, D)
    down_grad = down_grad.reshape(EXPERTS * SPLIT, FF // SPLIT, D)
    return layer_out, grad_tokens, grad_routing, gate_grad, up_grad, down_grad
```

```python
import jax
import jax.numpy as jnp
from jax import lax
from jax.sharding import PartitionSpec as P


def body(
    tokens,
    expert_ids,
    gate_weights,
    grad_output,
    gate_weight,
    up_weight,
    down_weight,
    swap_slot,
    slot_cap,
):
    n_expert = lax.axis_size("expert")
    n_group = lax.axis_size("dp")
    token_count, top_count = expert_ids.shape
    slot_count = slot_cap.shape[1]
    halves = n_group // slot_count
    width = tokens.shape[1]
    experts = n_expert * slot_count
    capacity = token_count * top_count // experts
    half_axis = n_expert // 2
    expert_range = jnp.arange(experts, dtype=jnp.int32)
    home_device = expert_range // slot_count
    local_slot = expert_range % slot_count
    was_moved = local_slot == swap_slot[home_device % half_axis]
    holder = jnp.where(was_moved, (home_device + half_axis) % n_expert, home_device)
    capacity_of = slot_cap[holder, local_slot]
    bucket = local_slot * n_expert + home_device
    flat_ids = expert_ids.reshape(-1)
    one_hot = (flat_ids[:, None] == expert_range[None, :]).astype(jnp.int32)
    earlier = jnp.cumsum(one_hot, axis=0) - one_hot
    rank_in = jnp.sum(earlier * one_hot, axis=1)
    is_kept = rank_in < jnp.sum(one_hot * capacity_of[None, :], axis=1)
    position = jnp.sum(one_hot * bucket[None, :], axis=1) * capacity + rank_in
    total_slots = experts * capacity
    slot_range = jnp.arange(total_slots, dtype=jnp.int32)
    slot_map = ((position[None, :] == slot_range[:, None]) & is_kept[None, :]).astype(jnp.bfloat16)
    token_map = jnp.sum(slot_map.reshape(total_slots, token_count, top_count), axis=2)
    send_rows = jnp.dot(token_map, tokens, preferred_element_type=jnp.float32).astype(jnp.bfloat16)
    slot_gate = jnp.dot(
        slot_map.astype(jnp.float32), gate_weights.reshape(-1), precision=lax.Precision.HIGHEST
    )
    picked_grads = jnp.dot(token_map, grad_output, preferred_element_type=jnp.float32)
    send_grads = (slot_gate[:, None] * picked_grads).astype(jnp.bfloat16)
    held_gate = gate_weight[0]
    held_up = up_weight[0]
    held_down = down_weight[0]
    sectioned_in = (
        lax.all_to_all(
            send_rows.reshape(slot_count, n_expert, capacity, width),
            "expert",
            split_axis=1,
            concat_axis=1,
            tiled=True,
        ),
        lax.all_to_all(
            send_grads.reshape(slot_count, n_expert, capacity, width),
            "expert",
            split_axis=1,
            concat_axis=1,
            tiled=True,
        ),
    )

    def spread_slots(values):
        tiled = jnp.broadcast_to(values[:, None], (slot_count, halves, n_expert, capacity, width))
        return tiled.reshape(n_group, n_expert * capacity, width)

    grouped = (
        lax.all_to_all(
            spread_slots(sectioned_in[0]), "dp", split_axis=0, concat_axis=0, tiled=True
        ),
        lax.all_to_all(
            spread_slots(sectioned_in[1]), "dp", split_axis=0, concat_axis=0, tiled=True
        ),
    )
    token_rows = grouped[0].reshape(-1, width)
    grads_in = grouped[1].reshape(-1, width)
    gate_pre = jnp.einsum("rk,fk->rf", token_rows, held_gate, preferred_element_type=jnp.float32)
    up_pre = jnp.einsum("rk,fk->rf", token_rows, held_up, preferred_element_type=jnp.float32)
    activation = (jax.nn.silu(gate_pre) * up_pre).astype(jnp.bfloat16)
    partial_out = jnp.einsum(
        "rf,fk->rk", activation, held_down, preferred_element_type=jnp.float32
    ).astype(jnp.bfloat16)
    grad_act = jnp.einsum("rk,fk->rf", grads_in, held_down, preferred_element_type=jnp.float32)
    down_result = jnp.einsum(
        "rf,rk->fk", activation, grads_in, preferred_element_type=jnp.float32
    ).astype(jnp.bfloat16)
    gate_sig = jax.nn.sigmoid(gate_pre)
    delta_gate = (grad_act * up_pre * gate_sig * (1.0 + gate_pre * (1.0 - gate_sig))).astype(
        jnp.bfloat16
    )
    delta_up = (grad_act * gate_pre * gate_sig).astype(jnp.bfloat16)
    gate_result = jnp.einsum(
        "rf,rk->fk", delta_gate, token_rows, preferred_element_type=jnp.float32
    ).astype(jnp.bfloat16)
    up_result = jnp.einsum(
        "rf,rk->fk", delta_up, token_rows, preferred_element_type=jnp.float32
    ).astype(jnp.bfloat16)
    partial_in = jnp.einsum("rf,fk->rk", delta_gate, held_gate, preferred_element_type=jnp.float32)
    partial_in = (
        partial_in + jnp.einsum("rf,fk->rk", delta_up, held_up, preferred_element_type=jnp.float32)
    ).astype(jnp.bfloat16)
    returned_group = (
        lax.all_to_all(
            partial_out.reshape(n_group, n_expert * capacity, width),
            "dp",
            split_axis=0,
            concat_axis=0,
            tiled=True,
        ),
        lax.all_to_all(
            partial_in.reshape(n_group, n_expert * capacity, width),
            "dp",
            split_axis=0,
            concat_axis=0,
            tiled=True,
        ),
    )

    def pair_sectioned(values):
        return jnp.sum(
            values.reshape(slot_count, halves, n_expert, capacity, width).astype(jnp.float32),
            axis=1,
        ).astype(jnp.bfloat16)

    returned = (
        lax.all_to_all(
            pair_sectioned(returned_group[0]), "expert", split_axis=1, concat_axis=1, tiled=True
        ),
        lax.all_to_all(
            pair_sectioned(returned_group[1]), "expert", split_axis=1, concat_axis=1, tiled=True
        ),
    )
    out_rows = returned[0].reshape(total_slots, width)
    in_rows = returned[1].reshape(total_slots, width)
    per_assign = jnp.einsum(
        "qa,qk->ak", slot_map, out_rows, preferred_element_type=jnp.float32
    ).reshape(token_count, top_count, width)
    layer_out = jnp.sum(gate_weights[:, :, None] * per_assign, axis=1).astype(jnp.bfloat16)
    grad_routing = jnp.sum(grad_output.astype(jnp.float32)[:, None, :] * per_assign, axis=2)
    grad_tokens = jnp.einsum(
        "qt,qk->tk", token_map, in_rows, preferred_element_type=jnp.float32
    ).astype(jnp.bfloat16)
    gate_result = gate_result[None]
    up_result = up_result[None]
    down_result = down_result[None]
    return (layer_out, grad_tokens, grad_routing, gate_result, up_result, down_result)


def solution(mesh):
    in_specs = (
        P(("expert", "dp"), None),
        P(("expert", "dp"), None),
        P(("expert", "dp"), None),
        P(("expert", "dp"), None),
        P(("expert", "dp"), None, None),
        P(("expert", "dp"), None, None),
        P(("expert", "dp"), None, None),
        P(),
        P(),
    )
    out_specs = (
        P(("expert", "dp"), None),
        P(("expert", "dp"), None),
        P(("expert", "dp"), None),
        P(("expert", "dp"), None, None),
        P(("expert", "dp"), None, None),
        P(("expert", "dp"), None, None),
    )
    return jax.shard_map(body, mesh=mesh, in_specs=in_specs, out_specs=out_specs, check_vma=False)
```

```python
import functools

import jax
import jax.numpy as jnp
from jax import lax
from jax.experimental import pallas as pl
from jax.experimental.pallas import tpu as pltpu
from jax.sharding import PartitionSpec as P

BF = jnp.bfloat16
F32 = jnp.float32
MESH = pl.DeviceIdType.MESH
SIDE = 4
CHIPS = SIDE**3
LANES = 128
NT = (((1,), (1,)), ((), ()))
NN = (((1,), (0,)), ((), ()))


def dot(a, b, dims):
    return lax.dot_general(a, b, dims, preferred_element_type=F32)


def offset_of(n):
    n2, n1, n0 = n // 16, (n // 4) % 4, n % 4
    return n1, n0, (n2 + n1 + n0) % 4


def kernel(groups, cap, idx, gate_q, row_of, gate_a, tok, grad, wg_hbm, wu_hbm, wd_hbm,
           lo, gt, gr, gg_hbm, ug_hbm, dg_hbm,
           send, recv, xs, ds, act, dgate, dup, scr_a, scr_b, own, other, part, ret,
           wg, wu, wd, act_t, dgate_t, dup_t, stage,
           send_sem, recv_sem, fwd_ssem, fwd_rsem, part_ssem, part_rsem, ret_ssem, ret_rsem, w_sem, out_sem):
    width = wg.shape[1]
    units = wg.shape[0]
    cols = width // LANES
    tokens = tok.shape[0]
    slots = CHIPS // groups
    half = slots * cap
    rows = 2 * half

    h = lax.axis_index("expert")
    d = lax.axis_index("dp")
    x, z, y, c = h // SIDE, h % SIDE, d // 2, d % 2
    sibling = {"expert": h, "dp": y * 2 + (1 - c)}

    def chip(n, sign):
        kx, kz, ky = offset_of(n)
        if sign < 0:
            kx, kz, ky = SIDE - kx, SIDE - kz, SIDE - ky
        return {"expert": ((x + kx) % SIDE) * SIDE + (z + kz) % SIDE, "dp": ((y + ky) % SIDE) * 2 + c}

    barrier = pltpu.get_barrier_semaphore()
    pl.semaphore_signal(barrier, inc=1, device_id=sibling, device_id_type=MESH)

    def greet(n, _):
        pl.semaphore_signal(barrier, inc=1, device_id=chip(n, 1), device_id_type=MESH)
        return 0

    lax.fori_loop(1, CHIPS, greet, 0)

    def weight_copy(i):
        return pltpu.make_async_copy((wg_hbm, wu_hbm, wd_hbm)[i].at[0], (wg, wu, wd)[i], w_sem.at[i])

    for i in range(3):
        weight_copy(i).start()

    def dispatch(n):
        return pltpu.make_async_remote_copy(
            src_ref=send.at[n], dst_ref=recv.at[0, n], send_sem=send_sem.at[n], recv_sem=recv_sem.at[n],
            device_id=chip(n, 1), device_id_type=MESH)

    def gather(n, put):
        for r in range(cap):
            q = n * cap + r
            t = idx[q]
            put(r, tok[t])
            put(cap + r, (gate_q[q] * grad[t].astype(F32)).astype(BF))

    def put_own(r, value):
        recv[0, 0, r] = value

    gather(0, put_own)

    pl.semaphore_wait(barrier, CHIPS)

    def send_rows(n, _):
        def put(r, value):
            send[n, r] = value
        gather(n, put)
        dispatch(n).start()
        return 0

    lax.fori_loop(1, CHIPS, send_rows, 0)

    def forward(g):
        at = pl.ds(g * slots, slots)
        return pltpu.make_async_remote_copy(
            src_ref=recv.at[0, at], dst_ref=recv.at[1, at], send_sem=fwd_ssem.at[g], recv_sem=fwd_rsem.at[g],
            device_id=sibling, device_id_type=MESH)

    def trade(g):
        at = pl.ds(g * slots, slots)
        return pltpu.make_async_remote_copy(
            src_ref=other.at[at], dst_ref=part.at[at], send_sem=part_ssem.at[g], recv_sem=part_rsem.at[g],
            device_id=sibling, device_id_type=MESH)

    def give_back(n):
        return pltpu.make_async_remote_copy(
            src_ref=own.at[n], dst_ref=ret.at[n], send_sem=ret_ssem.at[n], recv_sem=ret_rsem.at[n],
            device_id=chip(n, -1), device_id_type=MESH)

    def arrive(g):
        def one(n, _):
            dispatch(n).wait_recv()
            return 0
        lax.fori_loop(max(g * slots, 1), (g + 1) * slots, one, 0)
        forward(g).start()

    def compute(g):
        base = g * rows
        first = g * slots
        forward(g).wait_recv()
        if g == 0:
            for i in range(3):
                weight_copy(i).wait()
        for p in range(2):
            def spread(i, _):
                n0 = first + i * 16
                r0 = pl.multiple_of(base + p * half + i * 16 * cap, 16)
                for lo_row, scr, dst in ((0, scr_a, xs), (cap, scr_b, ds)):
                    value = recv[p, pl.ds(n0, 16), lo_row:lo_row + cap].astype(F32)
                    scr[pl.ds(0, 16 * cap * cols), :] = value.reshape(16 * cap * cols, LANES)
                    for j in range(cols):
                        dst[pl.ds(r0, 16 * cap), j * LANES:(j + 1) * LANES] = scr[
                            pl.ds(j, 16 * cap, stride=cols), :].astype(BF)
                return 0
            lax.fori_loop(0, slots // 16, spread, 0)
        here = pl.ds(base, rows)

        def hidden(n, _):
            f = pl.ds(pl.multiple_of(n * 256, 256), 256)
            gate_pre = dot(xs[here, :], wg[f, :], NT)
            up_pre = dot(xs[here, :], wu[f, :], NT)
            grad_act = dot(ds[here, :], wd[f, :], NT)
            sig = jax.nn.sigmoid(gate_pre)
            silu = gate_pre * sig
            act[here, f] = (silu * up_pre).astype(BF)
            dup[here, f] = (grad_act * silu).astype(BF)
            dgate[here, f] = (grad_act * up_pre * sig * (1.0 + gate_pre * (1.0 - sig))).astype(BF)
            return 0

        lax.fori_loop(0, units // 256, hidden, 0)

        def model(n, _):
            f = pl.ds(pl.multiple_of(n * 256, 256), 256)
            out = dot(act[here, :], wd[:, f], NN)
            back = dot(dgate[here, :], wg[:, f], NN) + dot(dup[here, :], wu[:, f], NN)
            for k in range(2):
                lanes = slice(k * LANES, (k + 1) * LANES)
                scr_a[pl.ds(n * 2 + k, rows, stride=cols), :] = out[:, lanes]
                scr_b[pl.ds(n * 2 + k, rows, stride=cols), :] = back[:, lanes]
            return 0

        lax.fori_loop(0, width // 256, model, 0)
        for p, dst in ((0, own), (1, other)):
            def pack(i, _):
                n0 = first + i * 16
                at = pl.ds(pl.multiple_of((p * half + i * 16 * cap) * cols, 16), 16 * cap * cols)
                for lo_row, scr in ((0, scr_a), (cap, scr_b)):
                    dst[pl.ds(n0, 16), lo_row:lo_row + cap] = scr[at, :].astype(BF).reshape(16, cap, cols, LANES)
                return 0
            lax.fori_loop(0, slots // 16, pack, 0)
        trade(g).start()

    def finish(g):
        trade(g).wait_recv()

        def one(n, _):
            total = (own[n].astype(F32) + part[n].astype(F32)).astype(BF)
            own[n] = total
            give_back(n).start()
            return 0

        if g == 0:
            ret[0] = (own[0].astype(F32) + part[0].astype(F32)).astype(BF)
        lax.fori_loop(max(g * slots, 1), (g + 1) * slots, one, 0)

    for step in range(groups + 2):
        if step < groups:
            arrive(step)
        if 1 <= step <= groups:
            compute(step - 1)
        if step >= 2:
            finish(step - 2)

    act_t[...] = act[...].T
    dgate_t[...] = dgate[...].T
    dup_t[...] = dup[...].T
    tile = stage.shape[3]

    def out_copy(i, k, n):
        return pltpu.make_async_copy(
            stage.at[k, i],
            (gg_hbm, ug_hbm, dg_hbm)[i].at[0, :, pl.ds(pl.multiple_of(n * tile, tile), tile)],
            out_sem.at[k, i])

    steps = width // tile
    for n in range(steps):
        k = n % 2
        f = slice(n * tile, (n + 1) * tile)
        for i, (left, right) in enumerate(((dgate_t, xs), (dup_t, xs), (act_t, ds))):
            if n >= 2:
                out_copy(i, k, n - 2).wait()
            stage[k, i] = dot(left[...], right[:, f], NN).astype(BF)
            out_copy(i, k, n).start()

    def drain(n, _):
        give_back(n).wait_recv()
        return 0

    lax.fori_loop(1, CHIPS, drain, 0)

    def combine(t, _):
        cot = grad[t].astype(F32)
        total = jnp.zeros((cols, LANES), F32)
        back = jnp.zeros((cols, LANES), F32)
        for k in range(2):
            a = 2 * t + k
            q = row_of[a]
            n = q // (2 * cap)
            r = q % (2 * cap)
            out_row = ret[n, r].astype(F32)
            total = total + gate_a[a] * out_row
            back = back + ret[n, r + cap].astype(F32)
            gr[pl.ds(a, 1), :] = jnp.sum(cot * out_row, axis=0, keepdims=True)
        lo[t] = total.astype(BF)
        gt[t] = back.astype(BF)
        return 0

    lax.fori_loop(0, tokens, combine, 0)

    def settle(n, _):
        dispatch(n).wait_send()
        give_back(n).wait_send()
        return 0

    lax.fori_loop(1, CHIPS, settle, 0)
    for g in range(groups):
        forward(g).wait_send()
        trade(g).wait_send()
    for n in range(max(steps - 2, 0), steps):
        for i in range(3):
            out_copy(i, n % 2, n).wait()


def body(tokens, expert_ids, gate_weights, grad_output, gate_weight, up_weight, down_weight, swap_slot, slot_cap):
    count, top = expert_ids.shape
    width = tokens.shape[1]
    units = gate_weight.shape[1]
    holders, per = slot_cap.shape
    experts = holders * per
    cap = count * top // experts
    assigns = count * top
    cols = width // LANES
    groups = 2
    slots = CHIPS // groups
    rows = 2 * slots * cap

    h = lax.axis_index("expert")
    d = lax.axis_index("dp")
    half = holders // 2
    moved = jnp.concatenate([swap_slot, swap_slot])[:, None] == jnp.arange(per, dtype=jnp.int32)[None, :]
    rolled = jnp.concatenate([slot_cap[half:], slot_cap[:half]], axis=0)
    capacity = jnp.where(moved, rolled, slot_cap).reshape(experts)
    ids = expert_ids.reshape(-1)
    gates = gate_weights.reshape(-1)
    a_range = jnp.arange(assigns, dtype=jnp.int32)
    rank = jnp.sum(((ids[:, None] == ids[None, :]) & (a_range[None, :] < a_range[:, None])).astype(jnp.int32), axis=1)
    my_cap = jnp.sum(
        jnp.where(ids[:, None] == jnp.arange(experts, dtype=jnp.int32)[None, :], capacity[None, :], 0), axis=1)
    kept = rank < my_cap
    kx = (ids // 16 + SIDE - h // SIDE) % SIDE
    kz = ((ids // 4) % 4 + SIDE - h % SIDE) % SIDE
    ky = (ids % 4 + SIDE - d // 2) % SIDE
    slot = ((ky + 2 * SIDE - kx - kz) % SIDE) * 16 + kx * 4 + kz
    position = slot * cap + rank
    row_of = slot * 2 * cap + rank
    gate_a = jnp.where(kept, gates, 0.0)
    match = position[None, :] == a_range[:, None]
    idx = jnp.sum(jnp.where(match, (a_range // top)[None, :], 0), axis=1)
    gate_q = jnp.sum(jnp.where(match, gate_a[None, :], 0.0), axis=1)

    smem = pl.BlockSpec(memory_space=pltpu.SMEM)
    vmem = pl.BlockSpec(memory_space=pltpu.VMEM)
    hbm = pl.BlockSpec(memory_space=pl.ANY)
    rows3 = jax.ShapeDtypeStruct((count, cols, LANES), BF)
    block = (CHIPS, 2 * cap, cols, LANES)
    total = 2 * CHIPS * cap
    weights = jax.ShapeDtypeStruct((1, units, width), BF)
    dma = pltpu.SemaphoreType.DMA
    lo, gt, gr, gg, ug, dg = pl.pallas_call(
        functools.partial(kernel, groups, cap),
        out_shape=(rows3, rows3, jax.ShapeDtypeStruct((assigns, LANES), F32), weights, weights, weights),
        in_specs=[smem] * 4 + [vmem] * 2 + [hbm] * 3,
        out_specs=(vmem, vmem, vmem, hbm, hbm, hbm),
        scratch_shapes=[
            pltpu.VMEM(block, BF),
            pltpu.VMEM((2,) + block, BF),
            pltpu.VMEM((total, width), BF),
            pltpu.VMEM((total, width), BF),
            pltpu.VMEM((total, units), BF),
            pltpu.VMEM((total, units), BF),
            pltpu.VMEM((total, units), BF),
            pltpu.VMEM((rows * cols, LANES), F32),
            pltpu.VMEM((rows * cols, LANES), F32),
            pltpu.VMEM(block, BF),
            pltpu.VMEM(block, BF),
            pltpu.VMEM(block, BF),
            pltpu.VMEM(block, BF),
            pltpu.VMEM((units, width), BF),
            pltpu.VMEM((units, width), BF),
            pltpu.VMEM((units, width), BF),
            pltpu.VMEM((units, total), BF),
            pltpu.VMEM((units, total), BF),
            pltpu.VMEM((units, total), BF),
            pltpu.VMEM((2, 3, units, 256), BF),
            dma((CHIPS,)),
            dma((CHIPS,)),
            dma((groups,)),
            dma((groups,)),
            dma((groups,)),
            dma((groups,)),
            dma((CHIPS,)),
            dma((CHIPS,)),
            dma((3,)),
            dma((2, 3)),
        ],
        compiler_params=pltpu.CompilerParams(
            collective_id=0, has_side_effects=True, vmem_limit_bytes=62 * 1024 * 1024),
        cost_estimate=pl.CostEstimate(
            flops=18 * total * units * width, bytes_accessed=12 * units * width, transcendentals=0),
    )(idx, gate_q, row_of, gate_a, tokens.reshape(count, cols, LANES), grad_output.reshape(count, cols, LANES),
      gate_weight, up_weight, down_weight)
    routing = jnp.where(kept, jnp.sum(gr, axis=1), 0.0).reshape(count, top)
    return lo.reshape(count, width), gt.reshape(count, width), routing, gg, ug, dg


def solution(mesh):
    flat = P(("expert", "dp"), None)
    cube = P(("expert", "dp"), None, None)
    return jax.shard_map(
        body,
        mesh=mesh,
        in_specs=(flat, flat, flat, flat, cube, cube, cube, P(), P()),
        out_specs=(flat, flat, flat, cube, cube, cube),
        check_vma=False,
    )
```

```python
import functools

import jax
import jax.numpy as jnp
from jax import lax
from jax.experimental import pallas as pl
from jax.experimental.pallas import tpu as pltpu
from jax.sharding import PartitionSpec as P

BF = jnp.bfloat16
F32 = jnp.float32
MESH = pl.DeviceIdType.MESH
SIDE = 4
CHIPS = SIDE**3
LANES = 128
NT = (((1,), (1,)), ((), ()))
NN = (((1,), (0,)), ((), ()))


def dot(a, b, dims):
    return lax.dot_general(a, b, dims, preferred_element_type=F32)


def offset_of(n):
    n2, n1, n0 = n // 16, (n // 4) % 4, n % 4
    return n1, n0, (n2 + n1 + n0) % 4


def route(x, z, y, cap, swap, slot_cap, ids, gates, itab, ftab, kept_at):
    tokens = ids.shape[0]
    count = 2 * tokens
    experts = slot_cap.shape[0] * slot_cap.shape[1]
    per, holders = slot_cap.shape[1], slot_cap.shape[0]
    lane_e = lax.broadcasted_iota(jnp.int32, (1, experts), 1)
    cap_row = jnp.zeros((1, experts), jnp.int32)
    for e in range(experts):
        home, s = e // per, e % per
        away = (home + holders // 2) % holders
        cap_e = jnp.where(swap[home % (holders // 2)] == s, slot_cap[away, s], slot_cap[home, s])
        cap_row = jnp.where(lane_e == e, cap_e, cap_row)
    ids_c = jnp.concatenate([ids[:, 0:1], ids[:, 1:2]], axis=0)
    gate_c = jnp.concatenate([gates[:, 0:1], gates[:, 1:2]], axis=0)
    at_c = lax.broadcasted_iota(jnp.int32, (count, 1), 0)
    at_r = lax.broadcasted_iota(jnp.int32, (1, count), 1)
    second_c, second_r = (at_c >= tokens).astype(jnp.int32), (at_r >= tokens).astype(jnp.int32)
    token_c = at_c - tokens * second_c
    key_c = 2 * token_c + second_c
    key_r = 2 * (at_r - tokens * second_r) + second_r
    same = at_c == at_r
    ids_r = jnp.sum(jnp.where(same, ids_c, 0), axis=0, keepdims=True)
    earlier = (ids_c == ids_r) & (key_r < key_c)
    rank = jnp.sum(earlier.astype(jnp.int32), axis=1, keepdims=True)
    room = jnp.sum(jnp.where(ids_c == lane_e, cap_row, 0), axis=1, keepdims=True)
    kept = (rank < room).astype(F32)
    kx = ((ids_c >> 4) + (SIDE - x)) & 3
    kz = (((ids_c >> 2) & 3) + (SIDE - z)) & 3
    ky = ((ids_c & 3) + (SIDE - y)) & 3
    slot = ((ky + 2 * SIDE - kx - kz) & 3) * 16 + kx * 4 + kz
    gate_c = gate_c * kept
    rank = jnp.minimum(rank, cap - 1)
    match = slot * cap + rank == at_r
    itab[...] = jnp.zeros_like(itab)
    ftab[...] = jnp.zeros_like(ftab)
    itab[0:1, 0:count] = jnp.minimum(jnp.sum(jnp.where(match, token_c, 0), axis=0, keepdims=True), tokens - 1)
    itab[1:2, 0:count] = jnp.sum(jnp.where(same, slot * 2 * cap + rank, 0), axis=0, keepdims=True)
    ftab[0:1, 0:count] = jnp.sum(jnp.where(match, gate_c, 0.0), axis=0, keepdims=True)
    ftab[1:2, 0:count] = jnp.sum(jnp.where(same, gate_c, 0.0), axis=0, keepdims=True)
    kept_at[...] = kept


def kernel(groups, cap, swap, slot_cap, ids, gates, tok, grad, wg_hbm, wu_hbm, wd_hbm,
           lo, gt, routing, gg_hbm, ug_hbm, dg_hbm,
           itab, ftab, itab_s, ftab_s, kept_at, inner, tok3, grad3, send, recv, xs, ds, act, dgate, dup, scr_a, scr_b, own, other, part, ret,
           wg, wu, wd, act_t, dgate_t, dup_t, stage,
           send_sem, recv_sem, fwd_ssem, fwd_rsem, part_ssem, part_rsem, ret_ssem, ret_rsem, w_sem, out_sem, tab_sem):
    width = wg.shape[1]
    units = wg.shape[0]
    cols = width // LANES
    tokens = tok.shape[0]
    assigns = 2 * tokens
    slots = CHIPS // groups
    half = slots * cap
    rows = 2 * half

    h = lax.axis_index("expert")
    d = lax.axis_index("dp")
    x, z, y, c = h // SIDE, h % SIDE, d // 2, d % 2
    sibling = {"expert": h, "dp": y * 2 + (1 - c)}

    def chip(n, sign):
        kx, kz, ky = offset_of(n)
        if sign < 0:
            kx, kz, ky = SIDE - kx, SIDE - kz, SIDE - ky
        return {"expert": ((x + kx) % SIDE) * SIDE + (z + kz) % SIDE, "dp": ((y + ky) % SIDE) * 2 + c}

    barrier = pltpu.get_barrier_semaphore()
    pl.semaphore_signal(barrier, inc=1, device_id=sibling, device_id_type=MESH)

    def greet(n, _):
        pl.semaphore_signal(barrier, inc=1, device_id=chip(n, 1), device_id_type=MESH)
        return 0

    lax.fori_loop(1, CHIPS, greet, 0)

    def weight_copy(i):
        return pltpu.make_async_copy((wg_hbm, wu_hbm, wd_hbm)[i].at[0], (wg, wu, wd)[i], w_sem.at[i])

    for i in range(3):
        weight_copy(i).start()

    def dispatch(n):
        return pltpu.make_async_remote_copy(
            src_ref=send.at[n], dst_ref=recv.at[0, n], send_sem=send_sem.at[n], recv_sem=recv_sem.at[n],
            device_id=chip(n, 1), device_id_type=MESH)

    route(x, z, y, cap, swap, slot_cap, ids, gates, itab, ftab, kept_at)
    tables = [
        pltpu.make_async_copy(itab, itab_s, tab_sem.at[0]),
        pltpu.make_async_copy(ftab, ftab_s, tab_sem.at[1]),
    ]
    for copy in tables:
        copy.start()
    for j in range(cols):
        lanes = slice(j * LANES, (j + 1) * LANES)
        scr_a[pl.ds(j, tokens, stride=cols), :] = tok[:, lanes].astype(F32)
        scr_b[pl.ds(j, tokens, stride=cols), :] = grad[:, lanes].astype(F32)
    tok3[...] = scr_a[pl.ds(0, tokens * cols), :].astype(BF).reshape(tokens, cols, LANES)
    grad3[...] = scr_b[pl.ds(0, tokens * cols), :].reshape(tokens, cols, LANES)
    for copy in tables:
        copy.wait()

    def gather(n, put):
        for r in range(cap):
            q = n * cap + r
            t = itab_s[0, q]
            put(r, tok3[t])
            put(cap + r, (ftab_s[0, q] * grad3[t]).astype(BF))

    def put_own(r, value):
        recv[0, 0, r] = value

    gather(0, put_own)

    pl.semaphore_wait(barrier, CHIPS)

    def send_rows(n, _):
        def put(r, value):
            send[n, r] = value
        gather(n, put)
        dispatch(n).start()
        return 0

    lax.fori_loop(1, CHIPS, send_rows, 0)

    def forward(g):
        at = pl.ds(g * slots, slots)
        return pltpu.make_async_remote_copy(
            src_ref=recv.at[0, at], dst_ref=recv.at[1, at], send_sem=fwd_ssem.at[g], recv_sem=fwd_rsem.at[g],
            device_id=sibling, device_id_type=MESH)

    def trade(g):
        at = pl.ds(g * slots, slots)
        return pltpu.make_async_remote_copy(
            src_ref=other.at[at], dst_ref=part.at[at], send_sem=part_ssem.at[g], recv_sem=part_rsem.at[g],
            device_id=sibling, device_id_type=MESH)

    def give_back(n):
        return pltpu.make_async_remote_copy(
            src_ref=own.at[n], dst_ref=ret.at[n], send_sem=ret_ssem.at[n], recv_sem=ret_rsem.at[n],
            device_id=chip(n, -1), device_id_type=MESH)

    def arrive(g):
        def one(n, _):
            dispatch(n).wait_recv()
            return 0
        lax.fori_loop(max(g * slots, 1), (g + 1) * slots, one, 0)
        forward(g).start()

    def compute(g):
        base = g * rows
        first = g * slots
        for p in range(2):
            if p == 1:
                forward(g).wait_recv()
            def spread(i, _):
                n0 = first + i * 16
                r0 = pl.multiple_of(base + p * half + i * 16 * cap, 16)
                for lo_row, scr, dst in ((0, scr_a, xs), (cap, scr_b, ds)):
                    value = recv[p, pl.ds(n0, 16), lo_row:lo_row + cap].astype(F32)
                    scr[pl.ds(0, 16 * cap * cols), :] = value.reshape(16 * cap * cols, LANES)
                    for j in range(cols):
                        dst[pl.ds(r0, 16 * cap), j * LANES:(j + 1) * LANES] = scr[
                            pl.ds(j, 16 * cap, stride=cols), :].astype(BF)
                return 0
            lax.fori_loop(0, slots // 16, spread, 0)
        if g == 0:
            for i in range(3):
                weight_copy(i).wait()
        here = pl.ds(base, rows)

        def hidden(n, _):
            f = pl.ds(pl.multiple_of(n * 256, 256), 256)
            gate_pre = dot(xs[here, :], wg[f, :], NT)
            up_pre = dot(xs[here, :], wu[f, :], NT)
            grad_act = dot(ds[here, :], wd[f, :], NT)
            sig = jax.nn.sigmoid(gate_pre)
            silu = gate_pre * sig
            act[here, f] = (silu * up_pre).astype(BF)
            dup[here, f] = (grad_act * silu).astype(BF)
            dgate[here, f] = (grad_act * up_pre * sig * (1.0 + gate_pre * (1.0 - sig))).astype(BF)
            return 0

        lax.fori_loop(0, units // 256, hidden, 0)

        def model(n, _):
            f = pl.ds(pl.multiple_of(n * 256, 256), 256)
            out = dot(act[here, :], wd[:, f], NN)
            back = dot(dgate[here, :], wg[:, f], NN) + dot(dup[here, :], wu[:, f], NN)
            for k in range(2):
                lanes = slice(k * LANES, (k + 1) * LANES)
                scr_a[pl.ds(n * 2 + k, rows, stride=cols), :] = out[:, lanes]
                scr_b[pl.ds(n * 2 + k, rows, stride=cols), :] = back[:, lanes]
            return 0

        lax.fori_loop(0, width // 256, model, 0)
        for p, dst in ((0, own), (1, other)):
            def pack(i, _):
                n0 = first + i * 16
                at = pl.ds(pl.multiple_of((p * half + i * 16 * cap) * cols, 16), 16 * cap * cols)
                for lo_row, scr in ((0, scr_a), (cap, scr_b)):
                    dst[pl.ds(n0, 16), lo_row:lo_row + cap] = scr[at, :].astype(BF).reshape(16, cap, cols, LANES)
                return 0
            lax.fori_loop(0, slots // 16, pack, 0)
        trade(g).start()

    def finish(g):
        trade(g).wait_recv()

        def one(n, _):
            total = (own[n].astype(F32) + part[n].astype(F32)).astype(BF)
            own[n] = total
            give_back(n).start()
            return 0

        if g == 0:
            ret[0] = (own[0].astype(F32) + part[0].astype(F32)).astype(BF)
        lax.fori_loop(max(g * slots, 1), (g + 1) * slots, one, 0)

    for step in range(groups):
        arrive(step)
        if step >= 1:
            finish(step - 1)
        compute(step)
    act_t[...] = act[...].T
    finish(groups - 1)
    dgate_t[...] = dgate[...].T
    dup_t[...] = dup[...].T
    tile = stage.shape[3]

    def out_copy(i, k, n):
        return pltpu.make_async_copy(
            stage.at[k, i],
            (gg_hbm, ug_hbm, dg_hbm)[i].at[0, :, pl.ds(pl.multiple_of(n * tile, tile), tile)],
            out_sem.at[k, i])

    steps = width // tile
    for n in range(steps):
        k = n % 2
        f = slice(n * tile, (n + 1) * tile)
        for i, (left, right) in enumerate(((dgate_t, xs), (dup_t, xs), (act_t, ds))):
            if n >= 2:
                out_copy(i, k, n - 2).wait()
            stage[k, i] = dot(left[...], right[:, f], NN).astype(BF)
            out_copy(i, k, n).start()

    def drain(n, _):
        give_back(n).wait_recv()
        return 0

    lax.fori_loop(1, CHIPS, drain, 0)

    def combine(t, _):
        cot = grad3[t]
        total = jnp.zeros((cols, LANES), F32)
        back = jnp.zeros((cols, LANES), F32)
        for k in range(2):
            a = k * tokens + t
            q = itab_s[1, a]
            n = q // (2 * cap)
            r = q % (2 * cap)
            out_row = ret[n, r].astype(F32)
            total = total + ftab_s[1, a] * out_row
            back = back + ret[n, r + cap].astype(F32)
            inner[pl.ds(a, 1), :] = jnp.sum(cot * out_row, axis=0, keepdims=True)
        at = pl.ds(pl.multiple_of(t * cols, cols), cols)
        scr_a[at, :] = total
        scr_b[at, :] = back
        return 0

    lax.fori_loop(0, tokens, combine, 0, unroll=8)
    for j in range(cols):
        lanes = slice(j * LANES, (j + 1) * LANES)
        lo[:, lanes] = scr_a[pl.ds(j, tokens, stride=cols), :].astype(BF)
        gt[:, lanes] = scr_b[pl.ds(j, tokens, stride=cols), :].astype(BF)
    product = jnp.where(kept_at[...] > 0.0, jnp.sum(inner[...], axis=1, keepdims=True), 0.0)
    routing[...] = jnp.concatenate([product[:tokens], product[tokens:]], axis=1)

    def settle(n, _):
        dispatch(n).wait_send()
        give_back(n).wait_send()
        return 0

    lax.fori_loop(1, CHIPS, settle, 0)
    for g in range(groups):
        forward(g).wait_send()
        trade(g).wait_send()
    for n in range(max(steps - 2, 0), steps):
        for i in range(3):
            out_copy(i, n % 2, n).wait()


def body(tokens, expert_ids, gate_weights, grad_output, gate_weight, up_weight, down_weight, swap_slot, slot_cap):
    count, top = expert_ids.shape
    width = tokens.shape[1]
    units = gate_weight.shape[1]
    holders, per = slot_cap.shape
    experts = holders * per
    cap = count * top // experts
    assigns = count * top
    cols = width // LANES
    groups = 4
    slots = CHIPS // groups
    rows = 2 * slots * cap

    smem = pl.BlockSpec(memory_space=pltpu.SMEM)
    vmem = pl.BlockSpec(memory_space=pltpu.VMEM)
    hbm = pl.BlockSpec(memory_space=pl.ANY)
    flat_rows = jax.ShapeDtypeStruct((count, width), BF)
    block = (CHIPS, 2 * cap, cols, LANES)
    total = 2 * CHIPS * cap
    weights = jax.ShapeDtypeStruct((1, units, width), BF)
    dma = pltpu.SemaphoreType.DMA
    return pl.pallas_call(
        functools.partial(kernel, groups, cap),
        out_shape=(flat_rows, flat_rows, jax.ShapeDtypeStruct((count, top), F32), weights, weights, weights),
        in_specs=[smem] * 2 + [vmem] * 4 + [hbm] * 3,
        out_specs=(vmem, vmem, vmem, hbm, hbm, hbm),
        scratch_shapes=[
            pltpu.VMEM((8, 384), jnp.int32),
            pltpu.VMEM((8, 384), F32),
            pltpu.SMEM((8, 384), jnp.int32),
            pltpu.SMEM((8, 384), F32),
            pltpu.VMEM((assigns, 1), F32),
            pltpu.VMEM((assigns, LANES), F32),
            pltpu.VMEM((count, cols, LANES), BF),
            pltpu.VMEM((count, cols, LANES), F32),
            pltpu.VMEM(block, BF),
            pltpu.VMEM((2,) + block, BF),
            pltpu.VMEM((total, width), BF),
            pltpu.VMEM((total, width), BF),
            pltpu.VMEM((total, units), BF),
            pltpu.VMEM((total, units), BF),
            pltpu.VMEM((total, units), BF),
            pltpu.VMEM((rows * cols, LANES), F32),
            pltpu.VMEM((rows * cols, LANES), F32),
            pltpu.VMEM(block, BF),
            pltpu.VMEM(block, BF),
            pltpu.VMEM(block, BF),
            pltpu.VMEM(block, BF),
            pltpu.VMEM((units, width), BF),
            pltpu.VMEM((units, width), BF),
            pltpu.VMEM((units, width), BF),
            pltpu.VMEM((units, total), BF),
            pltpu.VMEM((units, total), BF),
            pltpu.VMEM((units, total), BF),
            pltpu.VMEM((2, 3, units, 256), BF),
            dma((CHIPS,)),
            dma((CHIPS,)),
            dma((groups,)),
            dma((groups,)),
            dma((groups,)),
            dma((groups,)),
            dma((CHIPS,)),
            dma((CHIPS,)),
            dma((3,)),
            dma((2, 3)),
            dma((2,)),
        ],
        compiler_params=pltpu.CompilerParams(
            collective_id=0, has_side_effects=True, vmem_limit_bytes=62 * 1024 * 1024),
        cost_estimate=pl.CostEstimate(
            flops=18 * total * units * width, bytes_accessed=12 * units * width, transcendentals=0),
    )(swap_slot, slot_cap, expert_ids, gate_weights, tokens, grad_output, gate_weight, up_weight, down_weight)


def solution(mesh):
    flat = P(("expert", "dp"), None)
    cube = P(("expert", "dp"), None, None)
    return jax.shard_map(
        body,
        mesh=mesh,
        in_specs=(flat, flat, flat, flat, cube, cube, cube, P(), P()),
        out_specs=(flat, flat, flat, cube, cube, cube),
        check_vma=False,
    )
```

```python
import functools

import jax
import jax.numpy as jnp
from jax import lax
from jax.experimental import pallas as pl
from jax.experimental.pallas import tpu as pltpu
from jax.sharding import PartitionSpec as P

BF = jnp.bfloat16
F32 = jnp.float32
MESH = pl.DeviceIdType.MESH
SIDE = 4
CHIPS = SIDE**3
LANES = 128
NT = (((1,), (1,)), ((), ()))
NN = (((1,), (0,)), ((), ()))


def dot(a, b, dims):
    return lax.dot_general(a, b, dims, preferred_element_type=F32)


def offset_of(n):
    n2, n1, n0 = n // 16, (n // 4) % 4, n % 4
    return n1, n0, (n2 + n1 + n0) % 4


def route(x, z, y, cap, swap, slot_cap, ids, gates, itab, ftab):
    tokens = ids.shape[1]
    count = 2 * tokens
    per, holders = slot_cap.shape
    experts = per * holders
    lane_e = lax.broadcasted_iota(jnp.int32, (1, experts), 1)
    cap_row = jnp.zeros((1, experts), jnp.int32)
    for e in range(experts):
        home, s = e // per, e % per
        away = (home + holders // 2) % holders
        cap_e = jnp.where(swap[home % (holders // 2)] == s, slot_cap[s, away], slot_cap[s, home])
        cap_row = jnp.where(lane_e == e, cap_e, cap_row)
    at_c = lax.broadcasted_iota(jnp.int32, (count, 1), 0)
    at_r = lax.broadcasted_iota(jnp.int32, (1, count), 1)
    second_c, second_r = (at_c >= tokens).astype(jnp.int32), (at_r >= tokens).astype(jnp.int32)
    token_c = at_c - tokens * second_c
    key_c = 2 * token_c + second_c
    key_r = 2 * (at_r - tokens * second_r) + second_r
    mine = token_c == lax.broadcasted_iota(jnp.int32, (1, tokens), 1)

    def column(ref):
        value = jnp.where(second_c == 1, ref[1:2, :], ref[0:1, :])
        return jnp.sum(jnp.where(mine, value, jnp.zeros_like(value)), axis=1, keepdims=True)

    ids_c, gate_c = column(ids), column(gates)
    same = at_c == at_r
    ids_r = jnp.sum(jnp.where(same, ids_c, 0), axis=0, keepdims=True)
    earlier = (ids_c == ids_r) & (key_r < key_c)
    rank = jnp.sum(earlier.astype(jnp.int32), axis=1, keepdims=True)
    room = jnp.sum(jnp.where(ids_c == lane_e, cap_row, 0), axis=1, keepdims=True)
    kept = (rank < room).astype(F32)
    kx = ((ids_c >> 4) + (SIDE - x)) & 3
    kz = (((ids_c >> 2) & 3) + (SIDE - z)) & 3
    ky = ((ids_c & 3) + (SIDE - y)) & 3
    slot = ((ky + 2 * SIDE - kx - kz) & 3) * 16 + kx * 4 + kz
    gate_c = gate_c * kept
    rank = jnp.minimum(rank, cap - 1)
    match = slot * cap + rank == at_r
    itab[...] = jnp.zeros_like(itab)
    ftab[...] = jnp.zeros_like(ftab)
    itab[0:1, 0:count] = jnp.minimum(jnp.sum(jnp.where(match, token_c, 0), axis=0, keepdims=True), tokens - 1)
    itab[1:2, 0:count] = jnp.sum(jnp.where(same, slot * 2 * cap + rank, 0), axis=0, keepdims=True)
    ftab[0:1, 0:count] = jnp.sum(jnp.where(match, gate_c, 0.0), axis=0, keepdims=True)
    ftab[1:2, 0:count] = jnp.sum(jnp.where(same, gate_c, 0.0), axis=0, keepdims=True)
    ftab[2:3, 0:count] = jnp.sum(jnp.where(same, kept, 0.0), axis=0, keepdims=True)


def turning():
    row = lax.broadcasted_iota(jnp.int32, (256, 256), 0)
    column = lax.broadcasted_iota(jnp.int32, (256, 256), 1)
    return (((row & 15) << 4) + (row >> 4) == column).astype(F32).astype(BF)


def to_tiles(turn, left, right, rows):
    parts = []
    for j in range(16):
        lanes = slice(j * LANES, (j + 1) * LANES)
        parts.append(jnp.concatenate([left[rows, lanes], right[rows, lanes]], axis=1))
    return dot(turn[...], jnp.concatenate(parts, axis=0), NN)


def kernel(groups, cap, swap, slot_cap, ids, gates, tok, grad, wg_hbm, wu_hbm, wd_hbm,
           ret, itab, ftab, gg_hbm, ug_hbm, dg_hbm,
           itab_s, ftab_s, turn, tok3, grad3, send, recv, xs, ds, act, dgate, dup, ys, dxs, own, other, part,
           wg, wu, wd, act_t, dgate_t, dup_t, stage,
           send_sem, recv_sem, fwd_ssem, fwd_rsem, part_ssem, part_rsem, ret_ssem, ret_rsem, w_sem, out_sem, tab_sem):
    width = wg.shape[1]
    units = wg.shape[0]
    cols = width // LANES
    tokens = tok.shape[0]
    slots = CHIPS // groups
    half = slots * cap
    rows = 2 * half

    h = lax.axis_index("expert")
    d = lax.axis_index("dp")
    x, z, y, c = h // SIDE, h % SIDE, d // 2, d % 2
    sibling = {"expert": h, "dp": y * 2 + (1 - c)}

    def chip(n, sign):
        kx, kz, ky = offset_of(n)
        if sign < 0:
            kx, kz, ky = SIDE - kx, SIDE - kz, SIDE - ky
        return {"expert": ((x + kx) % SIDE) * SIDE + (z + kz) % SIDE, "dp": ((y + ky) % SIDE) * 2 + c}

    barrier = pltpu.get_barrier_semaphore()
    pl.semaphore_signal(barrier, inc=1, device_id=sibling, device_id_type=MESH)

    def greet(n, _):
        pl.semaphore_signal(barrier, inc=1, device_id=chip(n, 1), device_id_type=MESH)
        return 0

    lax.fori_loop(1, CHIPS, greet, 0)

    def weight_copy(i):
        return pltpu.make_async_copy((wg_hbm, wu_hbm, wd_hbm)[i].at[0], (wg, wu, wd)[i], w_sem.at[i])

    for i in range(3):
        weight_copy(i).start()

    def dispatch(n):
        return pltpu.make_async_remote_copy(
            src_ref=send.at[n], dst_ref=recv.at[0, n], send_sem=send_sem.at[n], recv_sem=recv_sem.at[n],
            device_id=chip(n, 1), device_id_type=MESH)

    route(x, z, y, cap, swap, slot_cap, ids, gates, itab, ftab)
    tables = [
        pltpu.make_async_copy(itab, itab_s, tab_sem.at[0]),
        pltpu.make_async_copy(ftab, ftab_s, tab_sem.at[1]),
    ]
    for copy in tables:
        copy.start()
    turn[...] = turning()
    for b in range(tokens // 16):
        at = slice(b * 16, (b + 1) * 16)
        tiles = to_tiles(turn, tok, grad, at)
        tok3[at] = tiles[:, :LANES].astype(BF).reshape(16, cols, LANES)
        grad3[at] = tiles[:, LANES:].reshape(16, cols, LANES)
    for copy in tables:
        copy.wait()

    def gather(n, put):
        for r in range(cap):
            q = n * cap + r
            t = itab_s[0, q]
            put(r, tok3[t])
            put(cap + r, (ftab_s[0, q] * grad3[t]).astype(BF))

    def put_own(r, value):
        recv[0, 0, r] = value

    gather(0, put_own)

    pl.semaphore_wait(barrier, CHIPS)

    def send_rows(n, _):
        def put(r, value):
            send[n, r] = value
        gather(n, put)
        dispatch(n).start()
        return 0

    lax.fori_loop(1, CHIPS, send_rows, 0)

    def forward(g):
        at = pl.ds(g * slots, slots)
        return pltpu.make_async_remote_copy(
            src_ref=recv.at[0, at], dst_ref=recv.at[1, at], send_sem=fwd_ssem.at[g], recv_sem=fwd_rsem.at[g],
            device_id=sibling, device_id_type=MESH)

    def trade(g):
        at = pl.ds(g * slots, slots)
        return pltpu.make_async_remote_copy(
            src_ref=other.at[at], dst_ref=part.at[at], send_sem=part_ssem.at[g], recv_sem=part_rsem.at[g],
            device_id=sibling, device_id_type=MESH)

    def give_back(n):
        return pltpu.make_async_remote_copy(
            src_ref=own.at[n], dst_ref=ret.at[n], send_sem=ret_ssem.at[n], recv_sem=ret_rsem.at[n],
            device_id=chip(n, -1), device_id_type=MESH)

    keep = pltpu.make_async_copy(own.at[0], ret.at[0], tab_sem.at[2])

    def arrive(g):
        def one(n, _):
            dispatch(n).wait_recv()
            return 0
        lax.fori_loop(max(g * slots, 1), (g + 1) * slots, one, 0)
        forward(g).start()

    def compute(g):
        base = g * rows
        first = g * slots
        for p in range(2):
            if p == 1:
                forward(g).wait_recv()
            def spread(i, _):
                r0 = base + p * half + i * 16 * cap
                value = recv[p, pl.ds(first + i * 16, 16)]
                left = value[:, :cap].reshape(16 * cap * cols, LANES)
                right = value[:, cap:].reshape(16 * cap * cols, LANES)
                for b in range(cap):
                    at = slice(b * 256, (b + 1) * 256)
                    pair = jnp.concatenate([left[at], right[at]], axis=1)
                    turned = dot(turn[...], pair, NN).astype(BF)
                    here = pl.ds(pl.multiple_of(r0 + b * 16, 16), 16)
                    for j in range(cols):
                        lanes = slice(j * LANES, (j + 1) * LANES)
                        xs[here, lanes] = turned[j * 16:(j + 1) * 16, :LANES]
                        ds[here, lanes] = turned[j * 16:(j + 1) * 16, LANES:]
                return 0
            lax.fori_loop(0, slots // 16, spread, 0)
        if g == 0:
            for i in range(3):
                weight_copy(i).wait()
        here = pl.ds(base, rows)

        def hidden(n, _):
            f = pl.ds(pl.multiple_of(n * 256, 256), 256)
            gate_pre = dot(xs[here, :], wg[f, :], NT)
            up_pre = dot(xs[here, :], wu[f, :], NT)
            grad_act = dot(ds[here, :], wd[f, :], NT)
            sig = jax.nn.sigmoid(gate_pre)
            silu = gate_pre * sig
            act[here, f] = (silu * up_pre).astype(BF)
            dup[here, f] = (grad_act * silu).astype(BF)
            dgate[here, f] = (grad_act * up_pre * sig * (1.0 + gate_pre * (1.0 - sig))).astype(BF)
            return 0

        lax.fori_loop(0, units // 256, hidden, 0)

        def model(n, _):
            f = pl.ds(pl.multiple_of(n * 256, 256), 256)
            out = dot(act[here, :], wd[:, f], NN)
            back = dot(dgate[here, :], wg[:, f], NN) + dot(dup[here, :], wu[:, f], NN)
            ys[:, f] = out.astype(BF)
            dxs[:, f] = back.astype(BF)
            return 0

        lax.fori_loop(0, width // 256, model, 0)
        for p, dst in ((0, own), (1, other)):
            def pack(i, _):
                n0 = first + i * 16
                r0 = p * half + i * 16 * cap
                tiles = [
                    to_tiles(turn, ys, dxs, pl.ds(pl.multiple_of(r0 + b * 16, 16), 16)).astype(BF) for b in range(cap)]
                for k in range(2):
                    lanes = slice(k * LANES, (k + 1) * LANES)
                    rows3 = jnp.concatenate([t[:, lanes] for t in tiles], axis=0)
                    dst[pl.ds(n0, 16), k * cap:(k + 1) * cap] = rows3.reshape(16, cap, cols, LANES)
                return 0
            lax.fori_loop(0, slots // 16, pack, 0)
        trade(g).start()

    def finish(g):
        trade(g).wait_recv()

        def one(n, _):
            own[n] = (own[n].astype(F32) + part[n].astype(F32)).astype(BF)
            give_back(n).start()
            return 0

        if g == 0:
            own[0] = (own[0].astype(F32) + part[0].astype(F32)).astype(BF)
            keep.start()
        lax.fori_loop(max(g * slots, 1), (g + 1) * slots, one, 0)

    for step in range(groups):
        arrive(step)
        if step >= 1:
            finish(step - 1)
        compute(step)
    act_t[...] = act[...].T
    finish(groups - 1)
    dgate_t[...] = dgate[...].T
    dup_t[...] = dup[...].T
    tile = stage.shape[3]

    def out_copy(i, k, n):
        return pltpu.make_async_copy(
            stage.at[k, i],
            (gg_hbm, ug_hbm, dg_hbm)[i].at[0, :, pl.ds(pl.multiple_of(n * tile, tile), tile)],
            out_sem.at[k, i])

    steps = width // tile
    for n in range(steps):
        k = n % 2
        f = slice(n * tile, (n + 1) * tile)
        for i, (left, right) in enumerate(((dgate_t, xs), (dup_t, xs), (act_t, ds))):
            if n >= 2:
                out_copy(i, k, n - 2).wait()
            stage[k, i] = dot(left[...], right[:, f], NN).astype(BF)
            out_copy(i, k, n).start()

    def drain(n, _):
        give_back(n).wait_recv()
        return 0

    lax.fori_loop(1, CHIPS, drain, 0)

    keep.wait()

    def settle(n, _):
        dispatch(n).wait_send()
        give_back(n).wait_send()
        return 0

    lax.fori_loop(1, CHIPS, settle, 0)
    for g in range(groups):
        forward(g).wait_send()
        trade(g).wait_send()
    for n in range(max(steps - 2, 0), steps):
        for i in range(3):
            out_copy(i, n % 2, n).wait()


def last_kernel(cap, pieces, grad, itab, ftab, ret_hbm, gg_in, ug_in, dg_in,
                lo, gt, routing, gg, ug, dg,
                itab_s, ftab_s, ret, turn, grad3, total3, back3, inner, tab_sem, ret_sem, out_sem):
    tokens, width = grad.shape
    cols = width // LANES
    rows = gg.shape[1] // pieces
    fetch = [pltpu.make_async_copy(itab, itab_s, tab_sem.at[0]), pltpu.make_async_copy(ftab, ftab_s, tab_sem.at[1]),
             pltpu.make_async_copy(ret_hbm, ret, ret_sem)]
    moves = [
        pltpu.make_async_copy(src.at[0, pl.ds(k * rows, rows)], dst.at[0, pl.ds(k * rows, rows)], out_sem.at[i, k])
        for i, (src, dst) in enumerate(((gg_in, gg), (ug_in, ug), (dg_in, dg))) for k in range(pieces)]
    for copy in fetch + moves:
        copy.start()
    turn[...] = turning()
    for b in range(tokens // 32):
        low, high = slice(b * 32, b * 32 + 16), slice(b * 32 + 16, b * 32 + 32)
        parts = []
        for j in range(cols):
            lanes = slice(j * LANES, (j + 1) * LANES)
            parts.append(jnp.concatenate([grad[low, lanes], grad[high, lanes]], axis=1))
        tiles = dot(turn[...], jnp.concatenate(parts, axis=0), NN)
        grad3[low] = tiles[:, :LANES].reshape(16, cols, LANES)
        grad3[high] = tiles[:, LANES:].reshape(16, cols, LANES)
    for copy in fetch:
        copy.wait()

    def combine(t, _):
        cot = grad3[t]
        total = jnp.zeros((cols, LANES), F32)
        back = jnp.zeros((cols, LANES), F32)
        for k in range(2):
            a = k * tokens + t
            q = itab_s[1, a]
            n = q // (2 * cap)
            r = q % (2 * cap)
            out_row = ret[n, r].astype(F32)
            total = total + ftab_s[1, a] * out_row
            back = back + ret[n, r + cap].astype(F32)
            product = jnp.sum(cot * out_row, axis=0, keepdims=True)
            inner[pl.ds(a, 1), :] = jnp.where(ftab_s[2, a] > 0.0, product, 0.0)
        total3[t] = total.astype(BF)
        back3[t] = back.astype(BF)
        return 0

    lax.fori_loop(0, tokens, combine, 0, unroll=8)
    for b in range(tokens // 16):
        at = slice(b * 16, (b + 1) * 16)
        pair = jnp.concatenate([total3[at].reshape(256, LANES), back3[at].reshape(256, LANES)], axis=1)
        turned = dot(turn[...], pair, NN).astype(BF)
        for j in range(cols):
            lanes = slice(j * LANES, (j + 1) * LANES)
            lo[at, lanes] = turned[j * 16:(j + 1) * 16, :LANES]
            gt[at, lanes] = turned[j * 16:(j + 1) * 16, LANES:]
    sums = jnp.sum(inner[...], axis=1, keepdims=True)
    spot = lax.broadcasted_iota(jnp.int32, (tokens, tokens), 0) == lax.broadcasted_iota(jnp.int32, (tokens, tokens), 1)
    for k in range(2):
        routing[k:k + 1, :] = jnp.sum(
            jnp.where(spot, sums[k * tokens:(k + 1) * tokens], 0.0), axis=0, keepdims=True)
    for copy in moves:
        copy.wait()


def body(tokens, expert_ids, gate_weights, grad_output, gate_weight, up_weight, down_weight, swap_slot, slot_cap):
    count, top = expert_ids.shape
    width = tokens.shape[1]
    units = gate_weight.shape[1]
    holders, per = slot_cap.shape
    experts = holders * per
    cap = count * top // experts
    assigns = count * top
    cols = width // LANES
    groups = 2
    pieces = 4
    slots = CHIPS // groups
    rows = 2 * slots * cap

    smem = pl.BlockSpec(memory_space=pltpu.SMEM)
    vmem = pl.BlockSpec(memory_space=pltpu.VMEM)
    hbm = pl.BlockSpec(memory_space=pl.ANY)
    flat_rows = jax.ShapeDtypeStruct((count, width), BF)
    block = (CHIPS, 2 * cap, cols, LANES)
    total = 2 * CHIPS * cap
    weights = jax.ShapeDtypeStruct((1, units, width), BF)
    dma = pltpu.SemaphoreType.DMA
    ret, itab, ftab, *grads = pl.pallas_call(
        functools.partial(kernel, groups, cap),
        out_shape=(jax.ShapeDtypeStruct(block, BF), jax.ShapeDtypeStruct((8, 384), jnp.int32),
                   jax.ShapeDtypeStruct((8, 384), F32), weights, weights, weights),
        in_specs=[smem] * 2 + [vmem] * 4 + [hbm] * 3,
        out_specs=(hbm, vmem, vmem, hbm, hbm, hbm),
        scratch_shapes=[
            pltpu.SMEM((8, 384), jnp.int32),
            pltpu.SMEM((8, 384), F32),
            pltpu.VMEM((256, 256), BF),
            pltpu.VMEM((count, cols, LANES), BF),
            pltpu.VMEM((count, cols, LANES), F32),
            pltpu.VMEM(block, BF),
            pltpu.VMEM((2,) + block, BF),
            pltpu.VMEM((total, width), BF),
            pltpu.VMEM((total, width), BF),
            pltpu.VMEM((total, units), BF),
            pltpu.VMEM((total, units), BF),
            pltpu.VMEM((total, units), BF),
            pltpu.VMEM((rows, width), BF),
            pltpu.VMEM((rows, width), BF),
            pltpu.VMEM(block, BF),
            pltpu.VMEM(block, BF),
            pltpu.VMEM(block, BF),
            pltpu.VMEM((units, width), BF),
            pltpu.VMEM((units, width), BF),
            pltpu.VMEM((units, width), BF),
            pltpu.VMEM((units, total), BF),
            pltpu.VMEM((units, total), BF),
            pltpu.VMEM((units, total), BF),
            pltpu.VMEM((2, 3, units, 256), BF),
            dma((CHIPS,)),
            dma((CHIPS,)),
            dma((groups,)),
            dma((groups,)),
            dma((groups,)),
            dma((groups,)),
            dma((CHIPS,)),
            dma((CHIPS,)),
            dma((3,)),
            dma((2, 3)),
            dma((3,)),
        ],
        compiler_params=pltpu.CompilerParams(
            collective_id=0, has_side_effects=True, vmem_limit_bytes=62 * 1024 * 1024),
        cost_estimate=pl.CostEstimate(
            flops=18 * total * units * width, bytes_accessed=12 * units * width, transcendentals=0),
    )(swap_slot, slot_cap.T, expert_ids.T, gate_weights.T, tokens, grad_output, gate_weight, up_weight, down_weight)
    lo, gt, routing, gg, ug, dg = pl.pallas_call(
        functools.partial(last_kernel, cap, pieces),
        out_shape=(flat_rows, flat_rows, jax.ShapeDtypeStruct((top, count), F32), weights, weights, weights),
        in_specs=[vmem] * 3 + [hbm] * 4,
        out_specs=(vmem, vmem, vmem, hbm, hbm, hbm),
        scratch_shapes=[
            pltpu.SMEM((8, 384), jnp.int32),
            pltpu.SMEM((8, 384), F32),
            pltpu.VMEM(block, BF),
            pltpu.VMEM((256, 256), BF),
            pltpu.VMEM((count, cols, LANES), F32),
            pltpu.VMEM((count, cols, LANES), BF),
            pltpu.VMEM((count, cols, LANES), BF),
            pltpu.VMEM((assigns, LANES), F32),
            dma((2,)),
            dma,
            dma((3, pieces)),
        ],
        compiler_params=pltpu.CompilerParams(vmem_limit_bytes=62 * 1024 * 1024),
        cost_estimate=pl.CostEstimate(flops=0, bytes_accessed=12 * units * width, transcendentals=0),
    )(grad_output, itab, ftab, ret, *grads)
    return lo, gt, routing.T, gg, ug, dg


def solution(mesh):
    flat = P(("expert", "dp"), None)
    cube = P(("expert", "dp"), None, None)
    return jax.shard_map(
        body,
        mesh=mesh,
        in_specs=(flat, flat, flat, flat, cube, cube, cube, P(), P()),
        out_specs=(flat, flat, flat, cube, cube, cube),
        check_vma=False,
    )
```

```python
import functools

import jax
import jax.numpy as jnp
from jax import lax
from jax.experimental import pallas as pl
from jax.experimental.pallas import tpu as pltpu
from jax.sharding import PartitionSpec as P

BF = jnp.bfloat16
F32 = jnp.float32
MESH = pl.DeviceIdType.MESH
SIDE = 4
CHIPS = SIDE**3
LANES = 128
NT = (((1,), (1,)), ((), ()))
NN = (((1,), (0,)), ((), ()))


def dot(a, b, dims):
    return lax.dot_general(a, b, dims, preferred_element_type=F32)


def offset_of(n):
    n2, n1, n0 = n // 16, (n // 4) % 4, n % 4
    return n1, n0, (n2 + n1 + n0) % 4


def route(x, z, y, cap, swap, slot_cap, ids, gates, itab, ftab):
    tokens = ids.shape[1]
    count = 2 * tokens
    per, holders = slot_cap.shape
    experts = per * holders
    lane_e = lax.broadcasted_iota(jnp.int32, (1, experts), 1)
    cap_row = jnp.zeros((1, experts), jnp.int32)
    for e in range(experts):
        home, s = e // per, e % per
        away = (home + holders // 2) % holders
        cap_e = jnp.where(swap[home % (holders // 2)] == s, slot_cap[s, away], slot_cap[s, home])
        cap_row = jnp.where(lane_e == e, cap_e, cap_row)
    at_c = lax.broadcasted_iota(jnp.int32, (count, 1), 0)
    at_r = lax.broadcasted_iota(jnp.int32, (1, count), 1)
    second_c, second_r = (at_c >= tokens).astype(jnp.int32), (at_r >= tokens).astype(jnp.int32)
    token_c = at_c - tokens * second_c
    key_c = 2 * token_c + second_c
    key_r = 2 * (at_r - tokens * second_r) + second_r
    mine = token_c == lax.broadcasted_iota(jnp.int32, (1, tokens), 1)

    def column(ref):
        value = jnp.where(second_c == 1, ref[1:2, :], ref[0:1, :])
        return jnp.sum(jnp.where(mine, value, jnp.zeros_like(value)), axis=1, keepdims=True)

    ids_c, gate_c = column(ids), column(gates)
    same = at_c == at_r
    ids_r = jnp.sum(jnp.where(same, ids_c, 0), axis=0, keepdims=True)
    earlier = (ids_c == ids_r) & (key_r < key_c)
    rank = jnp.sum(earlier.astype(jnp.int32), axis=1, keepdims=True)
    room = jnp.sum(jnp.where(ids_c == lane_e, cap_row, 0), axis=1, keepdims=True)
    kept = (rank < room).astype(F32)
    kx = ((ids_c >> 4) + (SIDE - x)) & 3
    kz = (((ids_c >> 2) & 3) + (SIDE - z)) & 3
    ky = ((ids_c & 3) + (SIDE - y)) & 3
    slot = ((ky + 2 * SIDE - kx - kz) & 3) * 16 + kx * 4 + kz
    gate_c = gate_c * kept
    rank = jnp.minimum(rank, cap - 1)
    match = slot * cap + rank == at_r
    itab[...] = jnp.zeros_like(itab)
    ftab[...] = jnp.zeros_like(ftab)
    itab[0:1, 0:count] = jnp.minimum(jnp.sum(jnp.where(match, token_c, 0), axis=0, keepdims=True), tokens - 1)
    itab[1:2, 0:count] = jnp.sum(jnp.where(same, slot * 2 * cap + rank, 0), axis=0, keepdims=True)
    ftab[0:1, 0:count] = jnp.sum(jnp.where(match, gate_c, 0.0), axis=0, keepdims=True)
    ftab[1:2, 0:count] = jnp.sum(jnp.where(same, gate_c, 0.0), axis=0, keepdims=True)
    for k in range(2):
        ftab[2 + k:3 + k, 0:tokens] = jnp.sum(
            jnp.where(mine & (second_c == k), kept, 0.0), axis=0, keepdims=True)


def turning():
    row = lax.broadcasted_iota(jnp.int32, (256, 256), 0)
    column = lax.broadcasted_iota(jnp.int32, (256, 256), 1)
    return (((row & 15) << 4) + (row >> 4) == column).astype(F32).astype(BF)


def to_tiles(turn, left, right, rows):
    parts = []
    for j in range(16):
        lanes = slice(j * LANES, (j + 1) * LANES)
        parts.append(jnp.concatenate([left[rows, lanes], right[rows, lanes]], axis=1))
    return dot(turn[...], jnp.concatenate(parts, axis=0), NN)


def kernel(groups, cap, swap, slot_cap, ids, gates, tok, grad, wg_hbm, wu_hbm, wd_hbm,
           ret, itab, ftab, gg_hbm, ug_hbm, dg_hbm,
           itab_s, ftab_s, turn, tok3, grad3, send, recv, xs, ds, act, dgate, dup, ys, dxs, own, other, part,
           wg, wu, wd, act_t, dgate_t, dup_t, stage,
           send_sem, recv_sem, fwd_ssem, fwd_rsem, part_ssem, part_rsem, ret_ssem, ret_rsem, w_sem, out_sem, tab_sem):
    width = wg.shape[1]
    units = wg.shape[0]
    cols = width // LANES
    tokens = tok.shape[0]
    slots = CHIPS // groups
    half = slots * cap
    rows = 2 * half

    h = lax.axis_index("expert")
    d = lax.axis_index("dp")
    x, z, y, c = h // SIDE, h % SIDE, d // 2, d % 2
    sibling = {"expert": h, "dp": y * 2 + (1 - c)}

    def chip(n, sign):
        kx, kz, ky = offset_of(n)
        if sign < 0:
            kx, kz, ky = SIDE - kx, SIDE - kz, SIDE - ky
        return {"expert": ((x + kx) % SIDE) * SIDE + (z + kz) % SIDE, "dp": ((y + ky) % SIDE) * 2 + c}

    barrier = pltpu.get_barrier_semaphore()
    pl.semaphore_signal(barrier, inc=1, device_id=sibling, device_id_type=MESH)

    def greet(n, _):
        pl.semaphore_signal(barrier, inc=1, device_id=chip(n, 1), device_id_type=MESH)
        return 0

    lax.fori_loop(1, CHIPS, greet, 0)

    def weight_copy(i):
        return pltpu.make_async_copy((wg_hbm, wu_hbm, wd_hbm)[i].at[0], (wg, wu, wd)[i], w_sem.at[i])

    for i in range(3):
        weight_copy(i).start()

    def dispatch(n):
        return pltpu.make_async_remote_copy(
            src_ref=send.at[n], dst_ref=recv.at[0, n], send_sem=send_sem.at[n], recv_sem=recv_sem.at[n],
            device_id=chip(n, 1), device_id_type=MESH)

    route(x, z, y, cap, swap, slot_cap, ids, gates, itab, ftab)
    tables = [
        pltpu.make_async_copy(itab, itab_s, tab_sem.at[0]),
        pltpu.make_async_copy(ftab, ftab_s, tab_sem.at[1]),
    ]
    for copy in tables:
        copy.start()
    turn[...] = turning()
    for b in range(tokens // 16):
        at = slice(b * 16, (b + 1) * 16)
        tiles = to_tiles(turn, tok, grad, at)
        tok3[at] = tiles[:, :LANES].astype(BF).reshape(16, cols, LANES)
        grad3[at] = tiles[:, LANES:].reshape(16, cols, LANES)
    for copy in tables:
        copy.wait()

    def gather(n, put):
        for r in range(cap):
            q = n * cap + r
            t = itab_s[0, q]
            put(r, tok3[t])
            put(cap + r, (ftab_s[0, q] * grad3[t]).astype(BF))

    def put_own(r, value):
        recv[0, 0, r] = value

    gather(0, put_own)

    pl.semaphore_wait(barrier, CHIPS)

    def send_rows(n, _):
        def put(r, value):
            send[n, r] = value
        gather(n, put)
        dispatch(n).start()
        return 0

    lax.fori_loop(1, CHIPS, send_rows, 0)

    def forward(g):
        at = pl.ds(g * slots, slots)
        return pltpu.make_async_remote_copy(
            src_ref=recv.at[0, at], dst_ref=recv.at[1, at], send_sem=fwd_ssem.at[g], recv_sem=fwd_rsem.at[g],
            device_id=sibling, device_id_type=MESH)

    def trade(g):
        at = pl.ds(g * slots, slots)
        return pltpu.make_async_remote_copy(
            src_ref=other.at[at], dst_ref=part.at[at], send_sem=part_ssem.at[g], recv_sem=part_rsem.at[g],
            device_id=sibling, device_id_type=MESH)

    def give_back(n):
        return pltpu.make_async_remote_copy(
            src_ref=own.at[n], dst_ref=ret.at[n], send_sem=ret_ssem.at[n], recv_sem=ret_rsem.at[n],
            device_id=chip(n, -1), device_id_type=MESH)

    keep = pltpu.make_async_copy(own.at[0], ret.at[0], tab_sem.at[2])

    def arrive(g):
        def one(n, _):
            dispatch(n).wait_recv()
            return 0
        lax.fori_loop(max(g * slots, 1), (g + 1) * slots, one, 0)
        forward(g).start()

    def compute(g):
        base = g * rows
        first = g * slots
        for p in range(2):
            if p == 1:
                forward(g).wait_recv()
            def spread(i, _):
                r0 = base + p * half + i * 16 * cap
                value = recv[p, pl.ds(first + i * 16, 16)]
                left = value[:, :cap].reshape(16 * cap * cols, LANES)
                right = value[:, cap:].reshape(16 * cap * cols, LANES)
                for b in range(cap):
                    at = slice(b * 256, (b + 1) * 256)
                    pair = jnp.concatenate([left[at], right[at]], axis=1)
                    turned = dot(turn[...], pair, NN).astype(BF)
                    here = pl.ds(pl.multiple_of(r0 + b * 16, 16), 16)
                    for j in range(cols):
                        lanes = slice(j * LANES, (j + 1) * LANES)
                        xs[here, lanes] = turned[j * 16:(j + 1) * 16, :LANES]
                        ds[here, lanes] = turned[j * 16:(j + 1) * 16, LANES:]
                return 0
            lax.fori_loop(0, slots // 16, spread, 0)
        if g == 0:
            for i in range(3):
                weight_copy(i).wait()
        here = pl.ds(base, rows)

        def hidden(n, _):
            f = pl.ds(pl.multiple_of(n * 256, 256), 256)
            gate_pre = dot(xs[here, :], wg[f, :], NT)
            up_pre = dot(xs[here, :], wu[f, :], NT)
            grad_act = dot(ds[here, :], wd[f, :], NT)
            sig = jax.nn.sigmoid(gate_pre)
            silu = gate_pre * sig
            act[here, f] = (silu * up_pre).astype(BF)
            dup[here, f] = (grad_act * silu).astype(BF)
            dgate[here, f] = (grad_act * up_pre * sig * (1.0 + gate_pre * (1.0 - sig))).astype(BF)
            return 0

        lax.fori_loop(0, units // 256, hidden, 0)

        def model(n, _):
            f = pl.ds(pl.multiple_of(n * 256, 256), 256)
            out = dot(act[here, :], wd[:, f], NN)
            back = dot(dgate[here, :], wg[:, f], NN) + dot(dup[here, :], wu[:, f], NN)
            ys[:, f] = out.astype(BF)
            dxs[:, f] = back.astype(BF)
            return 0

        lax.fori_loop(0, width // 256, model, 0)
        for p, dst in ((0, own), (1, other)):
            def pack(i, _):
                n0 = first + i * 16
                r0 = p * half + i * 16 * cap
                tiles = [
                    to_tiles(turn, ys, dxs, pl.ds(pl.multiple_of(r0 + b * 16, 16), 16)).astype(BF) for b in range(cap)]
                for k in range(2):
                    lanes = slice(k * LANES, (k + 1) * LANES)
                    rows3 = jnp.concatenate([t[:, lanes] for t in tiles], axis=0)
                    dst[pl.ds(n0, 16), k * cap:(k + 1) * cap] = rows3.reshape(16, cap, cols, LANES)
                return 0
            lax.fori_loop(0, slots // 16, pack, 0)
        trade(g).start()

    def finish(g):
        trade(g).wait_recv()

        def one(n, _):
            own[n] = (own[n].astype(F32) + part[n].astype(F32)).astype(BF)
            give_back(n).start()
            return 0

        if g == 0:
            own[0] = (own[0].astype(F32) + part[0].astype(F32)).astype(BF)
            keep.start()
        lax.fori_loop(max(g * slots, 1), (g + 1) * slots, one, 0)

    for step in range(groups):
        arrive(step)
        if step >= 1:
            finish(step - 1)
        compute(step)
    act_t[...] = act[...].T
    finish(groups - 1)
    dgate_t[...] = dgate[...].T
    dup_t[...] = dup[...].T
    tile = stage.shape[3]

    def out_copy(i, k, n):
        return pltpu.make_async_copy(
            stage.at[k, i],
            (gg_hbm, ug_hbm, dg_hbm)[i].at[0, :, pl.ds(pl.multiple_of(n * tile, tile), tile)],
            out_sem.at[k, i])

    steps = width // tile
    for n in range(steps):
        k = n % 2
        f = slice(n * tile, (n + 1) * tile)
        for i, (left, right) in enumerate(((dgate_t, xs), (dup_t, xs), (act_t, ds))):
            if n >= 2:
                out_copy(i, k, n - 2).wait()
            stage[k, i] = dot(left[...], right[:, f], NN).astype(BF)
            out_copy(i, k, n).start()

    def drain(n, _):
        give_back(n).wait_recv()
        return 0

    lax.fori_loop(1, CHIPS, drain, 0)

    keep.wait()

    def settle(n, _):
        dispatch(n).wait_send()
        give_back(n).wait_send()
        return 0

    lax.fori_loop(1, CHIPS, settle, 0)
    for g in range(groups):
        forward(g).wait_send()
        trade(g).wait_send()
    for n in range(max(steps - 2, 0), steps):
        for i in range(3):
            out_copy(i, n % 2, n).wait()


def last_kernel(cap, pieces, grad, itab, ftab, ret_hbm, gg_in, ug_in, dg_in,
                lo, gt, routing, gg, ug, dg,
                itab_s, ftab_s, ret, turn, grad3, total3, back3, inner, held, tab_sem, ret_sem, in_sem, out_sem):
    tokens, width = grad.shape
    cols = width // LANES
    rows = gg.shape[1] // pieces
    fetch = [pltpu.make_async_copy(itab, itab_s, tab_sem.at[0]), pltpu.make_async_copy(ftab, ftab_s, tab_sem.at[1]),
             pltpu.make_async_copy(ret_hbm, ret, ret_sem)]
    loads, stores = [], []
    for i, (src, dst) in enumerate(((gg_in, gg), (ug_in, ug), (dg_in, dg))):
        for k in range(pieces):
            at = pl.ds(k * rows, rows)
            loads.append(pltpu.make_async_copy(src.at[0, at], held.at[i, at], in_sem.at[i, k]))
            stores.append(pltpu.make_async_copy(held.at[i, at], dst.at[0, at], out_sem.at[i, k]))
    for copy in fetch + loads:
        copy.start()
    turn[...] = turning()
    for b in range(tokens // 32):
        low, high = slice(b * 32, b * 32 + 16), slice(b * 32 + 16, b * 32 + 32)
        parts = []
        for j in range(cols):
            lanes = slice(j * LANES, (j + 1) * LANES)
            parts.append(jnp.concatenate([grad[low, lanes], grad[high, lanes]], axis=1))
        tiles = dot(turn[...], jnp.concatenate(parts, axis=0), NN)
        grad3[low] = tiles[:, :LANES].reshape(16, cols, LANES)
        grad3[high] = tiles[:, LANES:].reshape(16, cols, LANES)
    for copy in fetch:
        copy.wait()

    def combine(t, _):
        cot = grad3[t]
        total = jnp.zeros((cols, LANES), F32)
        back = jnp.zeros((cols, LANES), F32)
        for k in range(2):
            a = k * tokens + t
            q = itab_s[1, a]
            out_row = ret[q].astype(F32)
            total = total + ftab_s[1, a] * out_row
            back = back + ret[q + cap].astype(F32)
            inner[pl.ds(a, 1), :] = jnp.sum(cot * out_row, axis=0, keepdims=True)
        total3[t] = total.astype(BF)
        back3[t] = back.astype(BF)
        return 0

    chunks = tokens // 32
    for chunk in range(chunks):
        lax.fori_loop(chunk * 32, (chunk + 1) * 32, combine, 0, unroll=8)
        for m in range(chunk * len(loads) // (chunks - 1), min((chunk + 1) * len(loads) // (chunks - 1), len(loads))):
            loads[m].wait()
            stores[m].start()
        for b in (2 * chunk, 2 * chunk + 1):
            at = slice(b * 16, (b + 1) * 16)
            pair = jnp.concatenate([total3[at].reshape(256, LANES), back3[at].reshape(256, LANES)], axis=1)
            turned = dot(turn[...], pair, NN).astype(BF)
            for j in range(cols):
                lanes = slice(j * LANES, (j + 1) * LANES)
                lo[at, lanes] = turned[j * 16:(j + 1) * 16, :LANES]
                gt[at, lanes] = turned[j * 16:(j + 1) * 16, LANES:]
    sums = jnp.sum(inner[...], axis=1, keepdims=True)
    spot = lax.broadcasted_iota(jnp.int32, (tokens, tokens), 0) == lax.broadcasted_iota(jnp.int32, (tokens, tokens), 1)
    for k in range(2):
        product = jnp.sum(jnp.where(spot, sums[k * tokens:(k + 1) * tokens], 0.0), axis=0, keepdims=True)
        routing[k:k + 1, :] = jnp.where(ftab[2 + k:3 + k, 0:tokens] > 0.0, product, 0.0)
    for copy in stores:
        copy.wait()


def body(tokens, expert_ids, gate_weights, grad_output, gate_weight, up_weight, down_weight, swap_slot, slot_cap):
    count, top = expert_ids.shape
    width = tokens.shape[1]
    units = gate_weight.shape[1]
    holders, per = slot_cap.shape
    experts = holders * per
    cap = count * top // experts
    assigns = count * top
    cols = width // LANES
    groups = 2
    pieces = 4
    slots = CHIPS // groups
    rows = 2 * slots * cap

    smem = pl.BlockSpec(memory_space=pltpu.SMEM)
    vmem = pl.BlockSpec(memory_space=pltpu.VMEM)
    hbm = pl.BlockSpec(memory_space=pl.ANY)
    flat_rows = jax.ShapeDtypeStruct((count, width), BF)
    block = (CHIPS, 2 * cap, cols, LANES)
    total = 2 * CHIPS * cap
    weights = jax.ShapeDtypeStruct((1, units, width), BF)
    dma = pltpu.SemaphoreType.DMA
    ret, itab, ftab, *grads = pl.pallas_call(
        functools.partial(kernel, groups, cap),
        out_shape=(jax.ShapeDtypeStruct(block, BF), jax.ShapeDtypeStruct((8, 384), jnp.int32),
                   jax.ShapeDtypeStruct((8, 384), F32), weights, weights, weights),
        in_specs=[smem] * 2 + [vmem] * 4 + [hbm] * 3,
        out_specs=(hbm, vmem, vmem, hbm, hbm, hbm),
        scratch_shapes=[
            pltpu.SMEM((8, 384), jnp.int32),
            pltpu.SMEM((8, 384), F32),
            pltpu.VMEM((256, 256), BF),
            pltpu.VMEM((count, cols, LANES), BF),
            pltpu.VMEM((count, cols, LANES), F32),
            pltpu.VMEM(block, BF),
            pltpu.VMEM((2,) + block, BF),
            pltpu.VMEM((total, width), BF),
            pltpu.VMEM((total, width), BF),
            pltpu.VMEM((total, units), BF),
            pltpu.VMEM((total, units), BF),
            pltpu.VMEM((total, units), BF),
            pltpu.VMEM((rows, width), BF),
            pltpu.VMEM((rows, width), BF),
            pltpu.VMEM(block, BF),
            pltpu.VMEM(block, BF),
            pltpu.VMEM(block, BF),
            pltpu.VMEM((units, width), BF),
            pltpu.VMEM((units, width), BF),
            pltpu.VMEM((units, width), BF),
            pltpu.VMEM((units, total), BF),
            pltpu.VMEM((units, total), BF),
            pltpu.VMEM((units, total), BF),
            pltpu.VMEM((2, 3, units, 256), BF),
            dma((CHIPS,)),
            dma((CHIPS,)),
            dma((groups,)),
            dma((groups,)),
            dma((groups,)),
            dma((groups,)),
            dma((CHIPS,)),
            dma((CHIPS,)),
            dma((3,)),
            dma((2, 3)),
            dma((3,)),
        ],
        compiler_params=pltpu.CompilerParams(
            collective_id=0, has_side_effects=True, vmem_limit_bytes=62 * 1024 * 1024),
        cost_estimate=pl.CostEstimate(
            flops=18 * total * units * width, bytes_accessed=12 * units * width, transcendentals=0),
    )(swap_slot, slot_cap.T, expert_ids.T, gate_weights.T, tokens, grad_output, gate_weight, up_weight, down_weight)
    lo, gt, routing, gg, ug, dg = pl.pallas_call(
        functools.partial(last_kernel, cap, pieces),
        out_shape=(flat_rows, flat_rows, jax.ShapeDtypeStruct((top, count), F32), weights, weights, weights),
        in_specs=[vmem] * 3 + [hbm] * 4,
        out_specs=(vmem, vmem, vmem, hbm, hbm, hbm),
        scratch_shapes=[
            pltpu.SMEM((8, 384), jnp.int32),
            pltpu.SMEM((8, 384), F32),
            pltpu.VMEM((2 * CHIPS * cap, cols, LANES), BF),
            pltpu.VMEM((256, 256), BF),
            pltpu.VMEM((count, cols, LANES), F32),
            pltpu.VMEM((count, cols, LANES), BF),
            pltpu.VMEM((count, cols, LANES), BF),
            pltpu.VMEM((assigns, LANES), F32),
            pltpu.VMEM((3, units, width), BF),
            dma((2,)),
            dma,
            dma((3, pieces)),
            dma((3, pieces)),
        ],
        compiler_params=pltpu.CompilerParams(vmem_limit_bytes=62 * 1024 * 1024),
        cost_estimate=pl.CostEstimate(flops=0, bytes_accessed=12 * units * width, transcendentals=0),
    )(grad_output, itab, ftab, ret.reshape(2 * CHIPS * cap, cols, LANES), *grads)
    return lo, gt, routing.T, gg, ug, dg


def solution(mesh):
    flat = P(("expert", "dp"), None)
    cube = P(("expert", "dp"), None, None)
    return jax.shard_map(
        body,
        mesh=mesh,
        in_specs=(flat, flat, flat, flat, cube, cube, cube, P(), P()),
        out_specs=(flat, flat, flat, cube, cube, cube),
        check_vma=False,
    )
```

```python
import functools

import jax
import jax.numpy as jnp
from jax import lax
from jax.experimental import pallas as pl
from jax.experimental.pallas import tpu as pltpu
from jax.sharding import PartitionSpec as P

BF = jnp.bfloat16
F32 = jnp.float32
MESH = pl.DeviceIdType.MESH
SIDE = 4
CHIPS = SIDE**3
LANES = 128
NT = (((1,), (1,)), ((), ()))
NN = (((1,), (0,)), ((), ()))


def dot(a, b, dims):
    return lax.dot_general(a, b, dims, preferred_element_type=F32)


def offset_of(n):
    n2, n1, n0 = n // 16, (n // 4) % 4, n % 4
    return n1, n0, (n2 + n1 + n0) % 4


def route(x, z, y, cap, swap, slot_cap, ids, gates, itab, ftab):
    tokens = ids.shape[1]
    count = 2 * tokens
    per, holders = slot_cap.shape
    experts = per * holders
    lane_e = lax.broadcasted_iota(jnp.int32, (1, experts), 1)
    cap_row = jnp.zeros((1, experts), jnp.int32)
    for e in range(experts):
        home, s = e // per, e % per
        away = (home + holders // 2) % holders
        cap_e = jnp.where(swap[home % (holders // 2)] == s, slot_cap[s, away], slot_cap[s, home])
        cap_row = jnp.where(lane_e == e, cap_e, cap_row)
    at_c = lax.broadcasted_iota(jnp.int32, (count, 1), 0)
    at_r = lax.broadcasted_iota(jnp.int32, (1, count), 1)
    second_c, second_r = (at_c >= tokens).astype(jnp.int32), (at_r >= tokens).astype(jnp.int32)
    token_c = at_c - tokens * second_c
    key_c = 2 * token_c + second_c
    key_r = 2 * (at_r - tokens * second_r) + second_r
    mine = token_c == lax.broadcasted_iota(jnp.int32, (1, tokens), 1)

    def column(ref):
        value = jnp.where(second_c == 1, ref[1:2, :], ref[0:1, :])
        return jnp.sum(jnp.where(mine, value, jnp.zeros_like(value)), axis=1, keepdims=True)

    ids_c, gate_c = column(ids), column(gates)
    same = at_c == at_r
    ids_r = jnp.sum(jnp.where(same, ids_c, 0), axis=0, keepdims=True)
    earlier = (ids_c == ids_r) & (key_r < key_c)
    rank = jnp.sum(earlier.astype(jnp.int32), axis=1, keepdims=True)
    room = jnp.sum(jnp.where(ids_c == lane_e, cap_row, 0), axis=1, keepdims=True)
    kept = (rank < room).astype(F32)
    kx = ((ids_c >> 4) + (SIDE - x)) & 3
    kz = (((ids_c >> 2) & 3) + (SIDE - z)) & 3
    ky = ((ids_c & 3) + (SIDE - y)) & 3
    slot = ((ky + 2 * SIDE - kx - kz) & 3) * 16 + kx * 4 + kz
    gate_c = gate_c * kept
    rank = jnp.minimum(rank, cap - 1)
    match = slot * cap + rank == at_r
    itab[...] = jnp.zeros_like(itab)
    ftab[...] = jnp.zeros_like(ftab)
    itab[0:1, 0:count] = jnp.minimum(jnp.sum(jnp.where(match, token_c, 0), axis=0, keepdims=True), tokens - 1)
    itab[1:2, 0:count] = jnp.sum(jnp.where(same, slot * 2 * cap + rank, 0), axis=0, keepdims=True)
    ftab[0:1, 0:count] = jnp.sum(jnp.where(match, gate_c, 0.0), axis=0, keepdims=True)
    ftab[1:2, 0:count] = jnp.sum(jnp.where(same, gate_c, 0.0), axis=0, keepdims=True)
    for k in range(2):
        ftab[2 + k:3 + k, 0:tokens] = jnp.sum(
            jnp.where(mine & (second_c == k), kept, 0.0), axis=0, keepdims=True)


def turning():
    row = lax.broadcasted_iota(jnp.int32, (256, 256), 0)
    column = lax.broadcasted_iota(jnp.int32, (256, 256), 1)
    return (((row & 15) << 4) + (row >> 4) == column).astype(F32).astype(BF)


def to_tiles(turn, left, right, rows):
    parts = []
    for j in range(16):
        lanes = slice(j * LANES, (j + 1) * LANES)
        parts.append(jnp.concatenate([left[rows, lanes], right[rows, lanes]], axis=1))
    return dot(turn[...], jnp.concatenate(parts, axis=0), NN)


def kernel(groups, cap, swap, slot_cap, ids, gates, tok, grad, wg_hbm, wu_hbm, wd_hbm,
           ret, itab, ftab, gg_hbm, ug_hbm, dg_hbm,
           itab_s, ftab_s, turn, tok3, grad3, send, recv, xs, ds, act, dgate, dup, ys, dxs, own, other, part,
           wg, wu, wd, act_t, dgate_t, dup_t, stage,
           send_sem, recv_sem, fwd_ssem, fwd_rsem, part_ssem, part_rsem, ret_ssem, ret_rsem, w_sem, out_sem, tab_sem, round_sem):
    width = wg.shape[1]
    units = wg.shape[0]
    cols = width // LANES
    tokens = tok.shape[0]
    slots = CHIPS // groups
    half = slots * cap
    rows = 2 * half

    h = lax.axis_index("expert")
    d = lax.axis_index("dp")
    x, z, y, c = h // SIDE, h % SIDE, d // 2, d % 2
    sibling = {"expert": h, "dp": y * 2 + (1 - c)}

    def chip(n, sign):
        kx, kz, ky = offset_of(n)
        if sign < 0:
            kx, kz, ky = SIDE - kx, SIDE - kz, SIDE - ky
        return {"expert": ((x + kx) % SIDE) * SIDE + (z + kz) % SIDE, "dp": ((y + ky) % SIDE) * 2 + c}

    barrier = pltpu.get_barrier_semaphore()
    pl.semaphore_signal(barrier, inc=1, device_id=sibling, device_id_type=MESH)

    def peer(i, j, k):
        return {"expert": ((x + i) % SIDE) * SIDE + (z + j) % SIDE, "dp": ((y + k) % SIDE) * 2 + c}

    for i in range(SIDE):
        for j in range(SIDE):
            if i or j:
                pl.semaphore_signal(barrier, inc=1, device_id=peer(i, j, 0), device_id_type=MESH)
    for k in range(1, SIDE):
        pl.semaphore_signal(barrier, inc=1, device_id=peer(0, 0, k), device_id_type=MESH)

    def weight_copy(i):
        return pltpu.make_async_copy((wg_hbm, wu_hbm, wd_hbm)[i].at[0], (wg, wu, wd)[i], w_sem.at[i])

    for i in range(3):
        weight_copy(i).start()

    def dispatch(n):
        return pltpu.make_async_remote_copy(
            src_ref=send.at[n], dst_ref=recv.at[0, n], send_sem=send_sem.at[n], recv_sem=recv_sem.at[n],
            device_id=chip(n, 1), device_id_type=MESH)

    route(x, z, y, cap, swap, slot_cap, ids, gates, itab, ftab)
    tables = [
        pltpu.make_async_copy(itab, itab_s, tab_sem.at[0]),
        pltpu.make_async_copy(ftab, ftab_s, tab_sem.at[1]),
    ]
    for copy in tables:
        copy.start()
    turn[...] = turning()
    for b in range(tokens // 16):
        at = slice(b * 16, (b + 1) * 16)
        tiles = to_tiles(turn, tok, grad, at)
        tok3[at] = tiles[:, :LANES].astype(BF).reshape(16, cols, LANES)
        grad3[at] = tiles[:, LANES:].reshape(16, cols, LANES)
    for copy in tables:
        copy.wait()

    def gather(n, put):
        for r in range(cap):
            q = n * cap + r
            t = itab_s[0, q]
            put(r, tok3[t])
            put(cap + r, (ftab_s[0, q] * grad3[t]).astype(BF))

    def put_own(r, value):
        recv[0, 0, r] = value

    gather(0, put_own)

    pl.semaphore_wait(barrier, 19)
    for k in range(1, SIDE):
        pl.semaphore_signal(round_sem, inc=1, device_id=peer(0, 0, k), device_id_type=MESH)
    pl.semaphore_wait(round_sem, 3)

    def send_rows(n, _):
        def put(r, value):
            send[n, r] = value
        gather(n, put)
        dispatch(n).start()
        return 0

    lax.fori_loop(1, CHIPS, send_rows, 0)

    def forward(g):
        at = pl.ds(g * slots, slots)
        return pltpu.make_async_remote_copy(
            src_ref=recv.at[0, at], dst_ref=recv.at[1, at], send_sem=fwd_ssem.at[g], recv_sem=fwd_rsem.at[g],
            device_id=sibling, device_id_type=MESH)

    def trade(g):
        at = pl.ds(g * slots, slots)
        return pltpu.make_async_remote_copy(
            src_ref=other.at[at], dst_ref=part.at[at], send_sem=part_ssem.at[g], recv_sem=part_rsem.at[g],
            device_id=sibling, device_id_type=MESH)

    def give_back(n):
        return pltpu.make_async_remote_copy(
            src_ref=own.at[n], dst_ref=ret.at[n], send_sem=ret_ssem.at[n], recv_sem=ret_rsem.at[n],
            device_id=chip(n, -1), device_id_type=MESH)

    keep = pltpu.make_async_copy(own.at[0], ret.at[0], tab_sem.at[2])

    def arrive(g):
        def one(n, _):
            dispatch(n).wait_recv()
            return 0
        lax.fori_loop(max(g * slots, 1), (g + 1) * slots, one, 0)
        forward(g).start()

    def compute(g):
        base = g * rows
        first = g * slots
        for p in range(2):
            if p == 1:
                forward(g).wait_recv()
            def spread(i, _):
                r0 = base + p * half + i * 16 * cap
                value = recv[p, pl.ds(first + i * 16, 16)]
                left = value[:, :cap].reshape(16 * cap * cols, LANES)
                right = value[:, cap:].reshape(16 * cap * cols, LANES)
                for b in range(cap):
                    at = slice(b * 256, (b + 1) * 256)
                    pair = jnp.concatenate([left[at], right[at]], axis=1)
                    turned = dot(turn[...], pair, NN).astype(BF)
                    here = pl.ds(pl.multiple_of(r0 + b * 16, 16), 16)
                    for j in range(cols):
                        lanes = slice(j * LANES, (j + 1) * LANES)
                        xs[here, lanes] = turned[j * 16:(j + 1) * 16, :LANES]
                        ds[here, lanes] = turned[j * 16:(j + 1) * 16, LANES:]
                return 0
            lax.fori_loop(0, slots // 16, spread, 0)
        if g == 0:
            for i in range(3):
                weight_copy(i).wait()
        here = pl.ds(base, rows)

        def hidden(n, _):
            f = pl.ds(pl.multiple_of(n * 256, 256), 256)
            gate_pre = dot(xs[here, :], wg[f, :], NT)
            up_pre = dot(xs[here, :], wu[f, :], NT)
            grad_act = dot(ds[here, :], wd[f, :], NT)
            sig = jax.nn.sigmoid(gate_pre)
            silu = gate_pre * sig
            act[here, f] = (silu * up_pre).astype(BF)
            dup[here, f] = (grad_act * silu).astype(BF)
            dgate[here, f] = (grad_act * up_pre * sig * (1.0 + gate_pre * (1.0 - sig))).astype(BF)
            return 0

        lax.fori_loop(0, units // 256, hidden, 0)

        def model(n, _):
            f = pl.ds(pl.multiple_of(n * 512, 256), 512)
            out = dot(act[here, :], wd[:, f], NN)
            back = dot(dgate[here, :], wg[:, f], NN) + dot(dup[here, :], wu[:, f], NN)
            ys[:, f] = out.astype(BF)
            dxs[:, f] = back.astype(BF)
            return 0

        lax.fori_loop(0, width // 512, model, 0)
        for p, dst in ((0, own), (1, other)):
            def pack(i, _):
                n0 = first + i * 16
                r0 = p * half + i * 16 * cap
                tiles = [
                    to_tiles(turn, ys, dxs, pl.ds(pl.multiple_of(r0 + b * 16, 16), 16)).astype(BF) for b in range(cap)]
                for k in range(2):
                    lanes = slice(k * LANES, (k + 1) * LANES)
                    rows3 = jnp.concatenate([t[:, lanes] for t in tiles], axis=0)
                    dst[pl.ds(n0, 16), k * cap:(k + 1) * cap] = rows3.reshape(16, cap, cols, LANES)
                return 0
            lax.fori_loop(0, slots // 16, pack, 0)
        trade(g).start()

    def finish(g):
        trade(g).wait_recv()

        def one(n, _):
            own[n] = (own[n].astype(F32) + part[n].astype(F32)).astype(BF)
            give_back(n).start()
            return 0

        if g == 0:
            own[0] = (own[0].astype(F32) + part[0].astype(F32)).astype(BF)
            keep.start()
        lax.fori_loop(max(g * slots, 1), (g + 1) * slots, one, 0)

    for step in range(groups):
        arrive(step)
        if step >= 1:
            finish(step - 1)
        compute(step)
    act_t[...] = act[...].T
    finish(groups - 1)
    dgate_t[...] = dgate[...].T
    dup_t[...] = dup[...].T
    tile = stage.shape[3]

    def out_copy(i, k, n):
        return pltpu.make_async_copy(
            stage.at[k, i],
            (gg_hbm, ug_hbm, dg_hbm)[i].at[0, :, pl.ds(pl.multiple_of(n * tile, tile), tile)],
            out_sem.at[k, i])

    steps = width // tile
    for n in range(steps):
        k = n % 2
        f = slice(n * tile, (n + 1) * tile)
        for i, (left, right) in enumerate(((dgate_t, xs), (dup_t, xs), (act_t, ds))):
            if n >= 2:
                out_copy(i, k, n - 2).wait()
            stage[k, i] = dot(left[...], right[:, f], NN).astype(BF)
            out_copy(i, k, n).start()

    def drain(n, _):
        give_back(n).wait_recv()
        return 0

    lax.fori_loop(1, CHIPS, drain, 0)

    keep.wait()

    def settle(n, _):
        dispatch(n).wait_send()
        give_back(n).wait_send()
        return 0

    lax.fori_loop(1, CHIPS, settle, 0)
    for g in range(groups):
        forward(g).wait_send()
        trade(g).wait_send()
    for n in range(max(steps - 2, 0), steps):
        for i in range(3):
            out_copy(i, n % 2, n).wait()


def last_kernel(cap, pieces, grad, itab, ftab, ret_hbm, gg_in, ug_in, dg_in,
                lo, gt, routing, gg, ug, dg,
                itab_s, ftab_s, ret, turn, grad3, total3, back3, inner, held, tab_sem, ret_sem, in_sem, out_sem):
    tokens, width = grad.shape
    cols = width // LANES
    rows = gg.shape[1] // pieces
    fetch = [pltpu.make_async_copy(itab, itab_s, tab_sem.at[0]), pltpu.make_async_copy(ftab, ftab_s, tab_sem.at[1]),
             pltpu.make_async_copy(ret_hbm, ret, ret_sem)]
    loads, stores = [], []
    for i, (src, dst) in enumerate(((gg_in, gg), (ug_in, ug), (dg_in, dg))):
        for k in range(pieces):
            at = pl.ds(k * rows, rows)
            loads.append(pltpu.make_async_copy(src.at[0, at], held.at[i, at], in_sem.at[i, k]))
            stores.append(pltpu.make_async_copy(held.at[i, at], dst.at[0, at], out_sem.at[i, k]))
    for copy in fetch + loads:
        copy.start()
    turn[...] = turning()
    for b in range(tokens // 32):
        low, high = slice(b * 32, b * 32 + 16), slice(b * 32 + 16, b * 32 + 32)
        parts = []
        for j in range(cols):
            lanes = slice(j * LANES, (j + 1) * LANES)
            parts.append(jnp.concatenate([grad[low, lanes], grad[high, lanes]], axis=1))
        tiles = dot(turn[...], jnp.concatenate(parts, axis=0), NN)
        grad3[low] = tiles[:, :LANES].reshape(16, cols, LANES)
        grad3[high] = tiles[:, LANES:].reshape(16, cols, LANES)
    for copy in fetch:
        copy.wait()

    def combine(t, _):
        cot = grad3[t]
        total = jnp.zeros((cols, LANES), F32)
        back = jnp.zeros((cols, LANES), F32)
        for k in range(2):
            a = k * tokens + t
            q = itab_s[1, a]
            out_row = ret[q].astype(F32)
            total = total + ftab_s[1, a] * out_row
            back = back + ret[q + cap].astype(F32)
            inner[pl.ds(a, 1), :] = jnp.sum(cot * out_row, axis=0, keepdims=True)
        total3[t] = total.astype(BF)
        back3[t] = back.astype(BF)
        return 0

    chunks = tokens // 32
    for chunk in range(chunks):
        lax.fori_loop(chunk * 32, (chunk + 1) * 32, combine, 0, unroll=8)
        for m in range(chunk * len(loads) // (chunks - 1), min((chunk + 1) * len(loads) // (chunks - 1), len(loads))):
            loads[m].wait()
            stores[m].start()
        for b in (2 * chunk, 2 * chunk + 1):
            at = slice(b * 16, (b + 1) * 16)
            pair = jnp.concatenate([total3[at].reshape(256, LANES), back3[at].reshape(256, LANES)], axis=1)
            turned = dot(turn[...], pair, NN).astype(BF)
            for j in range(cols):
                lanes = slice(j * LANES, (j + 1) * LANES)
                lo[at, lanes] = turned[j * 16:(j + 1) * 16, :LANES]
                gt[at, lanes] = turned[j * 16:(j + 1) * 16, LANES:]
    sums = jnp.sum(inner[...], axis=1, keepdims=True)
    spot = lax.broadcasted_iota(jnp.int32, (tokens, tokens), 0) == lax.broadcasted_iota(jnp.int32, (tokens, tokens), 1)
    for k in range(2):
        product = jnp.sum(jnp.where(spot, sums[k * tokens:(k + 1) * tokens], 0.0), axis=0, keepdims=True)
        routing[k:k + 1, :] = jnp.where(ftab[2 + k:3 + k, 0:tokens] > 0.0, product, 0.0)
    for copy in stores:
        copy.wait()


def body(tokens, expert_ids, gate_weights, grad_output, gate_weight, up_weight, down_weight, swap_slot, slot_cap):
    count, top = expert_ids.shape
    width = tokens.shape[1]
    units = gate_weight.shape[1]
    holders, per = slot_cap.shape
    experts = holders * per
    cap = count * top // experts
    assigns = count * top
    cols = width // LANES
    groups = 2
    pieces = 4
    slots = CHIPS // groups
    rows = 2 * slots * cap

    smem = pl.BlockSpec(memory_space=pltpu.SMEM)
    vmem = pl.BlockSpec(memory_space=pltpu.VMEM)
    hbm = pl.BlockSpec(memory_space=pl.ANY)
    flat_rows = jax.ShapeDtypeStruct((count, width), BF)
    block = (CHIPS, 2 * cap, cols, LANES)
    total = 2 * CHIPS * cap
    weights = jax.ShapeDtypeStruct((1, units, width), BF)
    dma = pltpu.SemaphoreType.DMA
    ret, itab, ftab, *grads = pl.pallas_call(
        functools.partial(kernel, groups, cap),
        out_shape=(jax.ShapeDtypeStruct(block, BF), jax.ShapeDtypeStruct((8, 384), jnp.int32),
                   jax.ShapeDtypeStruct((8, 384), F32), weights, weights, weights),
        in_specs=[smem] * 2 + [vmem] * 4 + [hbm] * 3,
        out_specs=(hbm, vmem, vmem, hbm, hbm, hbm),
        scratch_shapes=[
            pltpu.SMEM((8, 384), jnp.int32),
            pltpu.SMEM((8, 384), F32),
            pltpu.VMEM((256, 256), BF),
            pltpu.VMEM((count, cols, LANES), BF),
            pltpu.VMEM((count, cols, LANES), F32),
            pltpu.VMEM(block, BF),
            pltpu.VMEM((2,) + block, BF),
            pltpu.VMEM((total, width), BF),
            pltpu.VMEM((total, width), BF),
            pltpu.VMEM((total, units), BF),
            pltpu.VMEM((total, units), BF),
            pltpu.VMEM((total, units), BF),
            pltpu.VMEM((rows, width), BF),
            pltpu.VMEM((rows, width), BF),
            pltpu.VMEM(block, BF),
            pltpu.VMEM(block, BF),
            pltpu.VMEM(block, BF),
            pltpu.VMEM((units, width), BF),
            pltpu.VMEM((units, width), BF),
            pltpu.VMEM((units, width), BF),
            pltpu.VMEM((units, total), BF),
            pltpu.VMEM((units, total), BF),
            pltpu.VMEM((units, total), BF),
            pltpu.VMEM((2, 3, units, 256), BF),
            dma((CHIPS,)),
            dma((CHIPS,)),
            dma((groups,)),
            dma((groups,)),
            dma((groups,)),
            dma((groups,)),
            dma((CHIPS,)),
            dma((CHIPS,)),
            dma((3,)),
            dma((2, 3)),
            dma((3,)),
            pltpu.SemaphoreType.REGULAR,
        ],
        compiler_params=pltpu.CompilerParams(
            collective_id=0, has_side_effects=True, vmem_limit_bytes=62 * 1024 * 1024),
        cost_estimate=pl.CostEstimate(
            flops=18 * total * units * width, bytes_accessed=12 * units * width, transcendentals=0),
    )(swap_slot, slot_cap.T, expert_ids.T, gate_weights.T, tokens, grad_output, gate_weight, up_weight, down_weight)
    lo, gt, routing, gg, ug, dg = pl.pallas_call(
        functools.partial(last_kernel, cap, pieces),
        out_shape=(flat_rows, flat_rows, jax.ShapeDtypeStruct((top, count), F32), weights, weights, weights),
        in_specs=[vmem] * 3 + [hbm] * 4,
        out_specs=(vmem, vmem, vmem, hbm, hbm, hbm),
        scratch_shapes=[
            pltpu.SMEM((8, 384), jnp.int32),
            pltpu.SMEM((8, 384), F32),
            pltpu.VMEM((2 * CHIPS * cap, cols, LANES), BF),
            pltpu.VMEM((256, 256), BF),
            pltpu.VMEM((count, cols, LANES), F32),
            pltpu.VMEM((count, cols, LANES), BF),
            pltpu.VMEM((count, cols, LANES), BF),
            pltpu.VMEM((assigns, LANES), F32),
            pltpu.VMEM((3, units, width), BF),
            dma((2,)),
            dma,
            dma((3, pieces)),
            dma((3, pieces)),
        ],
        compiler_params=pltpu.CompilerParams(vmem_limit_bytes=62 * 1024 * 1024),
        cost_estimate=pl.CostEstimate(flops=0, bytes_accessed=12 * units * width, transcendentals=0),
    )(grad_output, itab, ftab, ret.reshape(2 * CHIPS * cap, cols, LANES), *grads)
    return lo, gt, routing.T, gg, ug, dg


def solution(mesh):
    flat = P(("expert", "dp"), None)
    cube = P(("expert", "dp"), None, None)
    return jax.shard_map(
        body,
        mesh=mesh,
        in_specs=(flat, flat, flat, flat, cube, cube, cube, P(), P()),
        out_specs=(flat, flat, flat, cube, cube, cube),
        check_vma=False,
    )
```

```python
import functools

import jax
import jax.numpy as jnp
from jax import lax
from jax.experimental import pallas as pl
from jax.experimental.pallas import tpu as pltpu
from jax.sharding import PartitionSpec as P

BF = jnp.bfloat16
F32 = jnp.float32
MESH = pl.DeviceIdType.MESH
SIDE = 4
CHIPS = SIDE**3
LANES = 128
NT = (((1,), (1,)), ((), ()))
NN = (((1,), (0,)), ((), ()))


def dot(a, b, dims):
    return lax.dot_general(a, b, dims, preferred_element_type=F32)


def offset_of(n):
    n2, n1, n0 = n // 16, (n // 4) % 4, n % 4
    return n1, n0, (n2 + n1 + n0) % 4


def route(x, z, y, cap, swap, slot_cap, ids, gates, itab, ftab):
    tokens = ids.shape[1]
    count = 2 * tokens
    per, holders = slot_cap.shape
    experts = per * holders
    lane_e = lax.broadcasted_iota(jnp.int32, (1, experts), 1)
    cap_row = jnp.zeros((1, experts), jnp.int32)
    for e in range(experts):
        home, s = e // per, e % per
        away = (home + holders // 2) % holders
        cap_e = jnp.where(swap[home % (holders // 2)] == s, slot_cap[s, away], slot_cap[s, home])
        cap_row = jnp.where(lane_e == e, cap_e, cap_row)
    at_c = lax.broadcasted_iota(jnp.int32, (count, 1), 0)
    at_r = lax.broadcasted_iota(jnp.int32, (1, count), 1)
    second_c, second_r = (at_c >= tokens).astype(jnp.int32), (at_r >= tokens).astype(jnp.int32)
    token_c = at_c - tokens * second_c
    key_c = 2 * token_c + second_c
    key_r = 2 * (at_r - tokens * second_r) + second_r
    mine = token_c == lax.broadcasted_iota(jnp.int32, (1, tokens), 1)

    def column(ref):
        value = jnp.where(second_c == 1, ref[1:2, :], ref[0:1, :])
        return jnp.sum(jnp.where(mine, value, jnp.zeros_like(value)), axis=1, keepdims=True)

    ids_c, gate_c = column(ids), column(gates)
    same = at_c == at_r
    ids_r = jnp.sum(jnp.where(same, ids_c, 0), axis=0, keepdims=True)
    earlier = (ids_c == ids_r) & (key_r < key_c)
    rank = jnp.sum(earlier.astype(jnp.int32), axis=1, keepdims=True)
    room = jnp.sum(jnp.where(ids_c == lane_e, cap_row, 0), axis=1, keepdims=True)
    kept = (rank < room).astype(F32)
    kx = ((ids_c >> 4) + (SIDE - x)) & 3
    kz = (((ids_c >> 2) & 3) + (SIDE - z)) & 3
    ky = ((ids_c & 3) + (SIDE - y)) & 3
    slot = ((ky + 2 * SIDE - kx - kz) & 3) * 16 + kx * 4 + kz
    gate_c = gate_c * kept
    rank = jnp.minimum(rank, cap - 1)
    match = slot * cap + rank == at_r
    itab[...] = jnp.zeros_like(itab)
    ftab[...] = jnp.zeros_like(ftab)
    itab[0:1, 0:count] = jnp.minimum(jnp.sum(jnp.where(match, token_c, 0), axis=0, keepdims=True), tokens - 1)
    itab[1:2, 0:count] = jnp.sum(jnp.where(same, slot * 2 * cap + rank, 0), axis=0, keepdims=True)
    ftab[0:1, 0:count] = jnp.sum(jnp.where(match, gate_c, 0.0), axis=0, keepdims=True)
    ftab[1:2, 0:count] = jnp.sum(jnp.where(same, gate_c, 0.0), axis=0, keepdims=True)
    for k in range(2):
        ftab[2 + k:3 + k, 0:tokens] = jnp.sum(
            jnp.where(mine & (second_c == k), kept, 0.0), axis=0, keepdims=True)


def turning():
    row = lax.broadcasted_iota(jnp.int32, (256, 256), 0)
    column = lax.broadcasted_iota(jnp.int32, (256, 256), 1)
    return (((row & 15) << 4) + (row >> 4) == column).astype(F32).astype(BF)


def to_tiles(turn, left, right, rows):
    parts = []
    for j in range(16):
        lanes = slice(j * LANES, (j + 1) * LANES)
        parts.append(jnp.concatenate([left[rows, lanes], right[rows, lanes]], axis=1))
    return dot(turn[...], jnp.concatenate(parts, axis=0), NN)


def kernel(groups, cap, swap, slot_cap, ids, gates, tok, grad, wg_hbm, wu_hbm, wd_hbm,
           ret, itab, ftab, gg_hbm, ug_hbm, dg_hbm,
           itab_s, ftab_s, turn, tok3, grad3, send, recv, xs, ds, act, dgate, dup, ys, dxs, own, other, part,
           wg, wu, wd, act_t, dgate_t, dup_t, stage,
           send_sem, recv_sem, fwd_ssem, fwd_rsem, part_ssem, part_rsem, ret_ssem, ret_rsem, w_sem, out_sem, tab_sem, round_sem):
    width = wg.shape[1]
    units = wg.shape[0]
    cols = width // LANES
    tokens = tok.shape[0]
    slots = CHIPS // groups
    half = slots * cap
    rows = 2 * half

    h = lax.axis_index("expert")
    d = lax.axis_index("dp")
    x, z, y, c = h // SIDE, h % SIDE, d // 2, d % 2
    sibling = {"expert": h, "dp": y * 2 + (1 - c)}

    def chip(n, sign):
        kx, kz, ky = offset_of(n)
        if sign < 0:
            kx, kz, ky = SIDE - kx, SIDE - kz, SIDE - ky
        return {"expert": ((x + kx) % SIDE) * SIDE + (z + kz) % SIDE, "dp": ((y + ky) % SIDE) * 2 + c}

    barrier = pltpu.get_barrier_semaphore()
    pl.semaphore_signal(barrier, inc=1, device_id=sibling, device_id_type=MESH)

    def peer(i, j, k):
        return {"expert": ((x + i) % SIDE) * SIDE + (z + j) % SIDE, "dp": ((y + k) % SIDE) * 2 + c}

    for i in range(SIDE):
        for j in range(SIDE):
            if i or j:
                pl.semaphore_signal(barrier, inc=1, device_id=peer(i, j, 0), device_id_type=MESH)
    for k in range(1, SIDE):
        pl.semaphore_signal(barrier, inc=1, device_id=peer(0, 0, k), device_id_type=MESH)

    def weight_copy(i):
        return pltpu.make_async_copy((wg_hbm, wu_hbm, wd_hbm)[i].at[0], (wg, wu, wd)[i], w_sem.at[i])

    for i in range(3):
        weight_copy(i).start()

    def dispatch(n):
        return pltpu.make_async_remote_copy(
            src_ref=send.at[n], dst_ref=recv.at[0, n], send_sem=send_sem.at[n], recv_sem=recv_sem.at[n],
            device_id=chip(n, 1), device_id_type=MESH)

    route(x, z, y, cap, swap, slot_cap, ids, gates, itab, ftab)
    tables = [
        pltpu.make_async_copy(itab, itab_s, tab_sem.at[0]),
        pltpu.make_async_copy(ftab, ftab_s, tab_sem.at[1]),
    ]
    for copy in tables:
        copy.start()
    turn[...] = turning()
    for b in range(tokens // 16):
        at = slice(b * 16, (b + 1) * 16)
        tiles = to_tiles(turn, tok, grad, at)
        tok3[at] = tiles[:, :LANES].astype(BF).reshape(16, cols, LANES)
        grad3[at] = tiles[:, LANES:].reshape(16, cols, LANES)
    for copy in tables:
        copy.wait()

    def gather(n, put):
        for r in range(cap):
            q = n * cap + r
            t = itab_s[0, q]
            put(r, tok3[t])
            put(cap + r, (ftab_s[0, q] * grad3[t]).astype(BF))

    def put_own(r, value):
        recv[0, 0, r] = value

    gather(0, put_own)

    pl.semaphore_wait(barrier, 19)
    for k in range(1, SIDE):
        pl.semaphore_signal(round_sem, inc=1, device_id=peer(0, 0, k), device_id_type=MESH)
    pl.semaphore_wait(round_sem, 3)

    def send_rows(n, _):
        def put(r, value):
            send[n, r] = value
        gather(n, put)
        dispatch(n).start()
        return 0

    lax.fori_loop(1, CHIPS, send_rows, 0)

    def forward(g):
        at = pl.ds(g * slots, slots)
        return pltpu.make_async_remote_copy(
            src_ref=recv.at[0, at], dst_ref=recv.at[1, at], send_sem=fwd_ssem.at[g], recv_sem=fwd_rsem.at[g],
            device_id=sibling, device_id_type=MESH)

    def trade(g):
        at = pl.ds(g * slots, slots)
        return pltpu.make_async_remote_copy(
            src_ref=other.at[at], dst_ref=part.at[at], send_sem=part_ssem.at[g], recv_sem=part_rsem.at[g],
            device_id=sibling, device_id_type=MESH)

    def give_back(n):
        return pltpu.make_async_remote_copy(
            src_ref=own.at[n], dst_ref=ret.at[n], send_sem=ret_ssem.at[n], recv_sem=ret_rsem.at[n],
            device_id=chip(n, -1), device_id_type=MESH)

    keep = pltpu.make_async_copy(own.at[0], ret.at[0], tab_sem.at[2])

    def arrive(g):
        def one(n, _):
            dispatch(n).wait_recv()
            return 0
        lax.fori_loop(max(g * slots, 1), (g + 1) * slots, one, 0)
        forward(g).start()

    def compute(g):
        base = g * rows
        first = g * slots
        for p in range(2):
            if p == 1:
                forward(g).wait_recv()
            def spread(i, _):
                r0 = base + p * half + i * 16 * cap
                value = recv[p, pl.ds(first + i * 16, 16)]
                left = value[:, :cap].reshape(16 * cap * cols, LANES)
                right = value[:, cap:].reshape(16 * cap * cols, LANES)
                for b in range(cap):
                    at = slice(b * 256, (b + 1) * 256)
                    pair = jnp.concatenate([left[at], right[at]], axis=1)
                    turned = dot(turn[...], pair, NN).astype(BF)
                    here = pl.ds(pl.multiple_of(r0 + b * 16, 16), 16)
                    for j in range(cols):
                        lanes = slice(j * LANES, (j + 1) * LANES)
                        xs[here, lanes] = turned[j * 16:(j + 1) * 16, :LANES]
                        ds[here, lanes] = turned[j * 16:(j + 1) * 16, LANES:]
                return 0
            lax.fori_loop(0, slots // 16, spread, 0)
        if g == 0:
            for i in range(3):
                weight_copy(i).wait()
        here = pl.ds(base, rows)

        def hidden(n, _):
            f = pl.ds(pl.multiple_of(n * 256, 256), 256)
            gate_pre = dot(xs[here, :], wg[f, :], NT)
            up_pre = dot(xs[here, :], wu[f, :], NT)
            grad_act = dot(ds[here, :], wd[f, :], NT)
            sig = jax.nn.sigmoid(gate_pre)
            silu = gate_pre * sig
            act[here, f] = (silu * up_pre).astype(BF)
            dup[here, f] = (grad_act * silu).astype(BF)
            dgate[here, f] = (grad_act * up_pre * sig * (1.0 + gate_pre * (1.0 - sig))).astype(BF)
            return 0

        lax.fori_loop(0, units // 256, hidden, 0)

        def model(n, _):
            f = pl.ds(pl.multiple_of(n * 512, 256), 512)
            out = dot(act[here, :], wd[:, f], NN)
            back = dot(dgate[here, :], wg[:, f], NN) + dot(dup[here, :], wu[:, f], NN)
            ys[:, f] = out.astype(BF)
            dxs[:, f] = back.astype(BF)
            return 0

        lax.fori_loop(0, width // 512, model, 0)
        for p, dst in ((0, own), (1, other)):
            def pack(i, _):
                n0 = first + i * 16
                r0 = p * half + i * 16 * cap
                tiles = [
                    to_tiles(turn, ys, dxs, pl.ds(pl.multiple_of(r0 + b * 16, 16), 16)).astype(BF) for b in range(cap)]
                for k in range(2):
                    lanes = slice(k * LANES, (k + 1) * LANES)
                    rows3 = jnp.concatenate([t[:, lanes] for t in tiles], axis=0)
                    dst[pl.ds(n0, 16), k * cap:(k + 1) * cap] = rows3.reshape(16, cap, cols, LANES)
                return 0
            lax.fori_loop(0, slots // 16, pack, 0)
        trade(g).start()

    def finish(g):
        trade(g).wait_recv()

        def one(n, _):
            own[n] = (own[n].astype(F32) + part[n].astype(F32)).astype(BF)
            give_back(n).start()
            return 0

        if g == 0:
            own[0] = (own[0].astype(F32) + part[0].astype(F32)).astype(BF)
            keep.start()
        lax.fori_loop(max(g * slots, 1), (g + 1) * slots, one, 0)

    for step in range(groups):
        arrive(step)
        if step >= 1:
            finish(step - 1)
        compute(step)
    act_t[...] = act[...].T
    finish(groups - 1)
    dgate_t[...] = dgate[...].T
    dup_t[...] = dup[...].T
    tile = stage.shape[3]

    def out_copy(i, k, n):
        return pltpu.make_async_copy(
            stage.at[k, i],
            (gg_hbm, ug_hbm, dg_hbm)[i].at[0, :, pl.ds(pl.multiple_of(n * tile, tile), tile)],
            out_sem.at[k, i])

    steps = width // tile
    for n in range(steps):
        k = n % 2
        f = slice(n * tile, (n + 1) * tile)
        for i, (left, right) in enumerate(((dgate_t, xs), (dup_t, xs), (act_t, ds))):
            if n >= 2:
                out_copy(i, k, n - 2).wait()
            stage[k, i] = dot(left[...], right[:, f], NN).astype(BF)
            out_copy(i, k, n).start()

    def drain(n, _):
        give_back(n).wait_recv()
        return 0

    lax.fori_loop(1, CHIPS, drain, 0)

    keep.wait()

    def settle(n, _):
        dispatch(n).wait_send()
        give_back(n).wait_send()
        return 0

    lax.fori_loop(1, CHIPS, settle, 0)
    for g in range(groups):
        forward(g).wait_send()
        trade(g).wait_send()
    for n in range(max(steps - 2, 0), steps):
        for i in range(3):
            out_copy(i, n % 2, n).wait()


def last_kernel(cap, pieces, grad, itab, ftab, ret_hbm, gg_in, ug_in, dg_in,
                lo, gt, routing, gg, ug, dg,
                itab_s, ftab_s, ret, turn, grad3, total3, back3, inner, held, tab_sem, ret_sem, in_sem, out_sem):
    tokens, width = grad.shape
    cols = width // LANES
    rows = gg.shape[1] // pieces
    fetch = [pltpu.make_async_copy(itab, itab_s, tab_sem.at[0]), pltpu.make_async_copy(ftab, ftab_s, tab_sem.at[1]),
             pltpu.make_async_copy(ret_hbm, ret, ret_sem)]
    loads, stores = [], []
    for i, (src, dst) in enumerate(((gg_in, gg), (ug_in, ug), (dg_in, dg))):
        for k in range(pieces):
            at = pl.ds(k * rows, rows)
            loads.append(pltpu.make_async_copy(src.at[0, at], held.at[i, at], in_sem.at[i, k]))
            stores.append(pltpu.make_async_copy(held.at[i, at], dst.at[0, at], out_sem.at[i, k]))
    for copy in fetch + loads:
        copy.start()
    turn[...] = turning()
    for b in range(tokens // 32):
        low, high = slice(b * 32, b * 32 + 16), slice(b * 32 + 16, b * 32 + 32)
        parts = []
        for j in range(cols):
            lanes = slice(j * LANES, (j + 1) * LANES)
            parts.append(jnp.concatenate([grad[low, lanes], grad[high, lanes]], axis=1))
        tiles = dot(turn[...], jnp.concatenate(parts, axis=0), NN)
        grad3[low] = tiles[:, :LANES].reshape(16, cols, LANES)
        grad3[high] = tiles[:, LANES:].reshape(16, cols, LANES)
    for copy in fetch:
        copy.wait()

    def combine(t, _):
        cot = grad3[t]
        total = jnp.zeros((cols, LANES), F32)
        back = jnp.zeros((cols, LANES), F32)
        for k in range(2):
            a = k * tokens + t
            q = itab_s[1, a]
            out_row = ret[q].astype(F32)
            total = total + ftab_s[1, a] * out_row
            back = back + ret[q + cap].astype(F32)
            inner[pl.ds(a, 1), :] = jnp.sum(cot * out_row, axis=0, keepdims=True)
        total3[t] = total.astype(BF)
        back3[t] = back.astype(BF)
        return 0

    chunks = tokens // 32
    for chunk in range(chunks):
        lax.fori_loop(chunk * 32, (chunk + 1) * 32, combine, 0, unroll=8)
        for m in range(chunk * len(loads) // (chunks - 1), min((chunk + 1) * len(loads) // (chunks - 1), len(loads))):
            loads[m].wait()
            stores[m].start()
        for b in (2 * chunk, 2 * chunk + 1):
            at = slice(b * 16, (b + 1) * 16)
            pair = jnp.concatenate([total3[at].reshape(256, LANES), back3[at].reshape(256, LANES)], axis=1)
            turned = dot(turn[...], pair, NN).astype(BF)
            for j in range(cols):
                lanes = slice(j * LANES, (j + 1) * LANES)
                lo[at, lanes] = turned[j * 16:(j + 1) * 16, :LANES]
                gt[at, lanes] = turned[j * 16:(j + 1) * 16, LANES:]
    sums = jnp.sum(inner[...], axis=1, keepdims=True)
    spot = lax.broadcasted_iota(jnp.int32, (tokens, tokens), 0) == lax.broadcasted_iota(jnp.int32, (tokens, tokens), 1)
    for k in range(2):
        product = jnp.sum(jnp.where(spot, sums[k * tokens:(k + 1) * tokens], 0.0), axis=0, keepdims=True)
        routing[k:k + 1, :] = jnp.where(ftab[2 + k:3 + k, 0:tokens] > 0.0, product, 0.0)
    for copy in stores:
        copy.wait()


def body(tokens, expert_ids, gate_weights, grad_output, gate_weight, up_weight, down_weight, swap_slot, slot_cap):
    count, top = expert_ids.shape
    width = tokens.shape[1]
    units = gate_weight.shape[1]
    holders, per = slot_cap.shape
    experts = holders * per
    cap = count * top // experts
    assigns = count * top
    cols = width // LANES
    groups = 4
    pieces = 4
    slots = CHIPS // groups
    rows = 2 * slots * cap

    smem = pl.BlockSpec(memory_space=pltpu.SMEM)
    vmem = pl.BlockSpec(memory_space=pltpu.VMEM)
    hbm = pl.BlockSpec(memory_space=pl.ANY)
    flat_rows = jax.ShapeDtypeStruct((count, width), BF)
    block = (CHIPS, 2 * cap, cols, LANES)
    total = 2 * CHIPS * cap
    weights = jax.ShapeDtypeStruct((1, units, width), BF)
    dma = pltpu.SemaphoreType.DMA
    ret, itab, ftab, *grads = pl.pallas_call(
        functools.partial(kernel, groups, cap),
        out_shape=(jax.ShapeDtypeStruct(block, BF), jax.ShapeDtypeStruct((8, 384), jnp.int32),
                   jax.ShapeDtypeStruct((8, 384), F32), weights, weights, weights),
        in_specs=[smem] * 2 + [vmem] * 4 + [hbm] * 3,
        out_specs=(hbm, vmem, vmem, hbm, hbm, hbm),
        scratch_shapes=[
            pltpu.SMEM((8, 384), jnp.int32),
            pltpu.SMEM((8, 384), F32),
            pltpu.VMEM((256, 256), BF),
            pltpu.VMEM((count, cols, LANES), BF),
            pltpu.VMEM((count, cols, LANES), F32),
            pltpu.VMEM(block, BF),
            pltpu.VMEM((2,) + block, BF),
            pltpu.VMEM((total, width), BF),
            pltpu.VMEM((total, width), BF),
            pltpu.VMEM((total, units), BF),
            pltpu.VMEM((total, units), BF),
            pltpu.VMEM((total, units), BF),
            pltpu.VMEM((rows, width), BF),
            pltpu.VMEM((rows, width), BF),
            pltpu.VMEM(block, BF),
            pltpu.VMEM(block, BF),
            pltpu.VMEM(block, BF),
            pltpu.VMEM((units, width), BF),
            pltpu.VMEM((units, width), BF),
            pltpu.VMEM((units, width), BF),
            pltpu.VMEM((units, total), BF),
            pltpu.VMEM((units, total), BF),
            pltpu.VMEM((units, total), BF),
            pltpu.VMEM((2, 3, units, 512), BF),
            dma((CHIPS,)),
            dma((CHIPS,)),
            dma((groups,)),
            dma((groups,)),
            dma((groups,)),
            dma((groups,)),
            dma((CHIPS,)),
            dma((CHIPS,)),
            dma((3,)),
            dma((2, 3)),
            dma((3,)),
            pltpu.SemaphoreType.REGULAR,
        ],
        compiler_params=pltpu.CompilerParams(
            collective_id=0, has_side_effects=True, vmem_limit_bytes=62 * 1024 * 1024),
        cost_estimate=pl.CostEstimate(
            flops=18 * total * units * width, bytes_accessed=12 * units * width, transcendentals=0),
    )(swap_slot, slot_cap.T, expert_ids.T, gate_weights.T, tokens, grad_output, gate_weight, up_weight, down_weight)
    lo, gt, routing, gg, ug, dg = pl.pallas_call(
        functools.partial(last_kernel, cap, pieces),
        out_shape=(flat_rows, flat_rows, jax.ShapeDtypeStruct((top, count), F32), weights, weights, weights),
        in_specs=[vmem] * 3 + [hbm] * 4,
        out_specs=(vmem, vmem, vmem, hbm, hbm, hbm),
        scratch_shapes=[
            pltpu.SMEM((8, 384), jnp.int32),
            pltpu.SMEM((8, 384), F32),
            pltpu.VMEM((2 * CHIPS * cap, cols, LANES), BF),
            pltpu.VMEM((256, 256), BF),
            pltpu.VMEM((count, cols, LANES), F32),
            pltpu.VMEM((count, cols, LANES), BF),
            pltpu.VMEM((count, cols, LANES), BF),
            pltpu.VMEM((assigns, LANES), F32),
            pltpu.VMEM((3, units, width), BF),
            dma((2,)),
            dma,
            dma((3, pieces)),
            dma((3, pieces)),
        ],
        compiler_params=pltpu.CompilerParams(vmem_limit_bytes=62 * 1024 * 1024),
        cost_estimate=pl.CostEstimate(flops=0, bytes_accessed=12 * units * width, transcendentals=0),
    )(grad_output, itab, ftab, ret.reshape(2 * CHIPS * cap, cols, LANES), *grads)
    return lo, gt, routing.T, gg, ug, dg


def solution(mesh):
    flat = P(("expert", "dp"), None)
    cube = P(("expert", "dp"), None, None)
    return jax.shard_map(
        body,
        mesh=mesh,
        in_specs=(flat, flat, flat, flat, cube, cube, cube, P(), P()),
        out_specs=(flat, flat, flat, cube, cube, cube),
        check_vma=False,
    )
```
